256 devices in a mesh: gx: 8 (over y, core), gy: 4 (over z_hi), gz: 8 (over x, z_lo).
Axes of the slice: x: 4, y: 4, z: 8 (z_hi: 4, z_lo: 2; z = z_hi * 2 + z_lo), core: 2. Of those that a mesh axis runs over, the one named last changes fastest.
Arguments:
- trial_block: float32 [96, 4, 8, 8, 1024], P(None, None, 'gx', 'gy', 'gz'), may hold values from -80 to 80
- site_shift: float32 [3, 4, 8, 8, 1024], P(None, None, 'gx', 'gy', 'gz'), may hold values from -0.32 to 0.32
- species: int32 [4, 8, 8, 1024], P(None, 'gx', 'gy', 'gz'), may hold values from 0 to 1
- neighbours: int32 [18, 4, 8, 8, 1024], P(None, None, 'gx', 'gy', 'gz'), may hold values from 131 to 6108, as said below
- counts: int32 [4, 8, 8, 1024], P(None, 'gx', 'gy', 'gz'), may hold values from 12 to 18
Outputs:
- residual: float32 [96, 4, 8, 8, 1024], P(None, None, 'gx', 'gy', 'gz')
- projected: float32 [32, 32], replicated
- residual_rms: float32 [32], replicated
The draws below stay inside these ranges and needn't reach their ends.
Inputs may be any that keep to these rules, and one draw needn't show every extreme that they name: Live slots of atom a hold its 12 nearest neighbours and those of its 6 second neighbours that lie within the cutoff, each once and in no fixed order, as the index (((s * 3 + ex) * 4 + ey) * 130 + ez) of sublattice s and cell (ex, ey, ez) of the owner's block extended by one cell on every side; a pair is listed at both of its atoms; the other slots hold the atom's own index.
All inputs are finite; a program needn't handle non-finite values.
Results may differ from the reference program's by a relative error of at most 0.0003.
Values sent between devices are 32-bit elements; how exact they have to be, the bound alone decides.
No kernel may reach another device: no remote copies, remote signals or barrier semaphores. Data moves between devices by JAX's collectives and lax.ppermute only.
A program may use at most 64 MiB of HBM per device.

```python
import math
import jax
import jax.numpy as jnp
import numpy as np
from jax import lax

CX = 1
CY = 2
CZ = 128
VECTORS = 32
NEIGHBOURS = 18
NX = 8
NY = 8
NZ = 1024


def lattice_tables():
    basis_half = [[0, 0, 0], [1, 1, 0], [1, 0, 1], [0, 1, 1]]
    step_list = []
    for first_axis in range(3):
        for second_axis in range(first_axis + 1, 3):
            for sign_first in (1, -1):
                for sign_second in (1, -1):
                    stepped = [0, 0, 0]
                    stepped[first_axis] = sign_first
                    stepped[second_axis] = sign_second
                    step_list.append(stepped)
    for axis_id in range(3):
        for sign_first in (2, -2):
            stepped = [0, 0, 0]
            stepped[axis_id] = sign_first
            step_list.append(stepped)
    cell_table = np.zeros((len(step_list), 4, 3), np.int32)
    target_table = np.zeros((len(step_list), 4), np.int32)
    for slot_id in range(len(step_list)):
        for sub_id in range(4):
            summed = [basis_half[sub_id][coord] + step_list[slot_id][coord] for coord in range(3)]
            cell_table[slot_id, sub_id] = [value_at // 2 for value_at in summed]
            target_table[slot_id, sub_id] = basis_half.index([value_at % 2 for value_at in summed])
    return (cell_table, target_table)


def neighbour_lists(key):
    bond_key = jax.random.fold_in(key, 101)
    order_key = jax.random.fold_in(key, 102)
    cell_table, target_table = lattice_tables()
    slot_total = cell_table.shape[0]
    lattice_shape = (4, NX, NY, NZ)
    sub_id = lax.broadcasted_iota(jnp.int32, lattice_shape, 0)
    cell_x = lax.broadcasted_iota(jnp.int32, lattice_shape, 1)
    cell_y = lax.broadcasted_iota(jnp.int32, lattice_shape, 2)
    cell_z = lax.broadcasted_iota(jnp.int32, lattice_shape, 3)
    local_x = cell_x % CX
    local_y = cell_y % CY
    local_z = cell_z % CZ
    offsets = jnp.asarray(cell_table)
    targets = jnp.asarray(target_table)[:, :, None, None, None]
    ext_x = local_x[None] + offsets[:, :, 0][:, :, None, None, None] + 1
    ext_y = local_y[None] + offsets[:, :, 1][:, :, None, None, None] + 1
    ext_z = local_z[None] + offsets[:, :, 2][:, :, None, None, None] + 1
    flat_index = ((targets * (CX + 2) + ext_x) * (CY + 2) + ext_y) * (CZ + 2) + ext_z
    bond_bits = jax.random.randint(bond_key, (3,) + lattice_shape, 0, 2, dtype=jnp.int32)
    corner = ((cell_x == 0) | (cell_x == NX - 1)) & ((cell_y == 0) | (cell_y == NY - 1)) & ((cell_z == 0) | (cell_z == NZ - 1))
    middle = ((cell_x == NX // 2) | (cell_x == NX // 2 - 1)) & ((cell_y == NY // 2) | (cell_y == NY // 2 - 1)) & ((cell_z == NZ // 2) | (cell_z == NZ // 2 - 1))
    bond_bits = jnp.where(corner[None], 1, jnp.where(middle[None], 0, bond_bits)).astype(jnp.int32)
    keeps = [bond_bits[0], jnp.roll(bond_bits[0], 1, axis=1), bond_bits[1], jnp.roll(bond_bits[1], 1, axis=2), bond_bits[2], jnp.roll(bond_bits[2], 1, axis=3)]
    alive = jnp.concatenate([jnp.ones((slot_total - 6,) + lattice_shape, jnp.int32), jnp.stack(keeps, 0)], 0)
    counted = jnp.sum(alive, 0).astype(jnp.int32)
    slot_ids = lax.broadcasted_iota(jnp.int32, (slot_total,) + lattice_shape, 0)
    scores = jax.random.randint(order_key, (slot_total,) + lattice_shape, 0, 2 ** 20, dtype=jnp.int32) * 32 + slot_ids + (1 - alive) * 2 ** 26
    ordering = jnp.argsort(scores, axis=0)
    listing = jnp.take_along_axis(flat_index, ordering, 0)
    alive_sorted = jnp.take_along_axis(alive, ordering, 0)
    own_index = ((sub_id * (CX + 2) + local_x + 1) * (CY + 2) + local_y + 1) * (CZ + 2) + local_z + 1
    listing = jnp.where(alive_sorted == 1, listing, own_index[None])
    return (listing.astype(jnp.int32), counted)


def draw_neighbours(key, part):
    listing, counted = neighbour_lists(key)
    return listing


def draw_counts(key, part):
    listing, counted = neighbour_lists(key)
    return counted


def draw_trial_block(key, part):
    key = jax.random.fold_in(key, 7)
    value_key, rough_key = jax.random.split(key, 2)
    lattice_shape = (4, NX, NY, NZ)
    ramp = (lax.broadcasted_iota(jnp.float32, lattice_shape, 1) / NX + lax.broadcasted_iota(jnp.float32, lattice_shape, 2) / NY + lax.broadcasted_iota(jnp.float32, lattice_shape, 3) / NZ) / 3.0
    rough = jax.random.uniform(rough_key, lattice_shape, jnp.float32)
    values = jnp.clip(jax.random.normal(value_key, (3, VECTORS) + lattice_shape, jnp.float32), -4.0, 4.0)
    scales = 10.0 ** (0.24 * ramp + 0.8 * rough)
    return jnp.reshape(values * scales[None, None], (3 * VECTORS,) + lattice_shape).astype(jnp.float32)


def place_ends(array, stream_key, low, largest):
    spot = [jax.random.randint(jax.random.fold_in(stream_key, axis), (), 0, length) for axis, length in enumerate(array.shape)]
    widest = array.shape.index(max(array.shape))
    neighbour = spot[:widest] + [(spot[widest] + 1) % array.shape[widest]] + spot[widest + 1:]
    return array.at[tuple(spot)].set(low).at[tuple(neighbour)].set(largest)


def block_scale(key, shape, cuts, smallest, high):
    level, own = 1.0, jax.random.fold_in(key, 6)
    for position, blocks in cuts:
        heights = jnp.exp(jax.random.uniform(jax.random.fold_in(own, position), (blocks,), jnp.float32, smallest / len(cuts), high / len(cuts)))
        level = level * jnp.repeat(heights, shape[position] // blocks).reshape([-1 if axis == position else 1 for axis in range(len(shape))])
    return level


def centred(stream_key, extent, width, most, shards=(), held_as=jnp.bfloat16):
    drawn = width * jax.random.normal(stream_key, extent, jnp.float32)
    if shards:
        drawn = drawn * block_scale(stream_key, extent, shards, -0.22, 0.18)
    return jnp.clip(drawn, -most, most).astype(held_as)


def setup_inputs(seed: int = 0) -> dict:
    key_list = jax.random.split(jax.random.key(seed), 6)
    trial_block = draw_trial_block(jax.random.fold_in(key_list[5], 71), 0)
    site_shift = centred(key_list[1], (3, 4, NX, NY, NZ), 0.08, 0.32, ((2, 8), (3, 4), (4, 8)), jnp.float32)
    species = place_ends(jax.random.randint(key_list[2], (4, NX, NY, NZ), 0, 2), jax.random.fold_in(key_list[2], 1), 0, 1).astype(jnp.int32)
    neighbours = draw_neighbours(jax.random.fold_in(key_list[5], 71), 0)
    counts = draw_counts(jax.random.fold_in(key_list[5], 71), 0)
    return dict(trial_block=trial_block, site_shift=site_shift, species=species, neighbours=neighbours, counts=counts)


lattice = 3.52
nearest = 3.52 / math.sqrt(2.0)
density_rate = 5.0
repulse_rate = 9.0
epsilon = 1e-06

def basis_bits(sub_id):
    along_x = ((sub_id == 1) | (sub_id == 2)).astype(jnp.int32)
    along_y = ((sub_id == 1) | (sub_id == 3)).astype(jnp.int32)
    along_z = ((sub_id == 2) | (sub_id == 3)).astype(jnp.int32)
    return (along_x, along_y, along_z)

def site_params(species):
    alloy = (species == 1).astype(jnp.float32)
    return (0.1 - 0.03 * alloy, 3.0 - 0.8 * alloy, 0.35 - 0.05 * alloy)

def radial_terms(distance, living, pair_here, pair_there):
    scaled = distance / nearest - 1.0
    density = living * jnp.exp(-density_rate * scaled)
    dens_first = -(density_rate / nearest) * density
    dens_second = (density_rate / nearest) ** 2 * density
    potential = living * pair_here * pair_there * jnp.exp(-repulse_rate * scaled)
    pot_first = -(repulse_rate / nearest) * potential
    pot_second = (repulse_rate / nearest) ** 2 * potential
    return (density, dens_first, dens_second, pot_first, pot_second)

def embed_slopes(rho, embedding):
    root_rho = jnp.sqrt(rho)
    return (-embedding / (2.0 * root_rho), embedding / (4.0 * rho * root_rho))

def pair_update(image, difference, projection, direction_s, distance_s, dens_first, dens_second, pot_first, pot_second, mixing):
    radial = pot_second - pot_first / distance_s + mixing * (dens_second - dens_first / distance_s)
    transverse = (pot_first + mixing * dens_first) / distance_s
    return image + radial[None, None] * direction_s[:, None, :] * projection[None] + transverse[None, None] * difference

def embed_update(image, direction_s, dens_first, amp_there, amp_here, weighted, weighted_there):
    coupled = amp_there[None] * weighted + amp_here[None] * weighted_there
    return image + dens_first[None, None] * direction_s[:, None, :] * coupled[None]

def project_block(gram, mixed):
    highest = lax.Precision.HIGHEST
    lower_factor = jnp.linalg.cholesky(gram)
    identity = jnp.eye(gram.shape[0], dtype=gram.dtype)
    inverse = jax.scipy.linalg.solve_triangular(lower_factor, identity, lower=True)
    raw_block = jnp.dot(jnp.dot(inverse, mixed, precision=highest), inverse.T, precision=highest)
    projected = 0.5 * (raw_block + raw_block.T)
    right_side = jnp.dot(inverse.T, projected, precision=highest)
    return (inverse, projected, right_side)

def reference(trial_block, site_shift, species, neighbours, counts):
    highest = lax.Precision.HIGHEST
    lattice_shape = (4, NX, NY, NZ)
    atom_total = 4 * NX * NY * NZ
    sub_id = lax.broadcasted_iota(jnp.int32, lattice_shape, 0).reshape(atom_total)
    cell_x = lax.broadcasted_iota(jnp.int32, lattice_shape, 1).reshape(atom_total)
    cell_y = lax.broadcasted_iota(jnp.int32, lattice_shape, 2).reshape(atom_total)
    cell_z = lax.broadcasted_iota(jnp.int32, lattice_shape, 3).reshape(atom_total)
    amplitude, embedding, pair_coef = site_params(species.reshape(atom_total))
    shifts = site_shift.reshape(3, atom_total)
    vectors = trial_block.reshape(3, VECTORS, atom_total)
    lists = neighbours.reshape(NEIGHBOURS, atom_total).astype(jnp.int32)
    live_count = counts.reshape(atom_total)
    ext_z = CZ + 2
    plane = (CY + 2) * ext_z
    volume = (CX + 2) * plane
    here_bits = basis_bits(sub_id)

    def geometry(slot_id):
        listed = lists[slot_id]
        living = (slot_id < live_count).astype(jnp.float32)
        sub_other = listed // volume
        remain = listed % volume
        off_x = remain // plane - 1 - cell_x % CX
        remain = remain % plane
        off_y = remain // ext_z - 1 - cell_y % CY
        off_z = remain % ext_z - 1 - cell_z % CZ
        partner = ((sub_other * NX + (cell_x + off_x) % NX) * NY + (cell_y + off_y) % NY) * NZ + (cell_z + off_z) % NZ
        partner = partner.astype(jnp.int32)
        there_bits = basis_bits(sub_other)
        half_steps = jnp.stack([2 * off_x + there_bits[0] - here_bits[0], 2 * off_y + there_bits[1] - here_bits[1], 2 * off_z + there_bits[2] - here_bits[2]], 0).astype(jnp.float32)
        separation = 0.5 * lattice * half_steps + shifts[:, partner] - shifts
        distance = jnp.sqrt(lax.optimization_barrier(jnp.sum(separation * separation, 0)))
        distance = jnp.where(living > 0, distance, nearest)
        direction = separation / distance[None]
        parts = radial_terms(distance, living, pair_coef, pair_coef[partner])
        return (partner, direction, distance, parts)

    def density_step(slot_id, summed):
        partner, direction, distance, parts = geometry(slot_id)
        return summed + amplitude[partner] * parts[0]
    rho = lax.fori_loop(0, NEIGHBOURS, density_step, jnp.zeros((atom_total,), jnp.float32))
    fprime, fsecond = embed_slopes(rho, embedding)

    def tangent_step(slot_id, running):
        tangent, image = running
        partner, direction, distance, parts = geometry(slot_id)
        density, dens_first, dens_second, pot_first, pot_second = parts
        amp_there = amplitude[partner]
        difference = vectors - vectors[:, :, partner]
        projection = lax.optimization_barrier(jnp.sum(direction[:, None, :] * difference, 0))
        tangent = tangent + (amp_there * dens_first)[None] * projection
        mixing = fprime * amp_there + fprime[partner] * amplitude
        image = pair_update(image, difference, projection, direction, distance, dens_first, dens_second, pot_first, pot_second, mixing)
        return (tangent, image)
    start = (jnp.zeros((VECTORS, atom_total), jnp.float32), jnp.zeros((3, VECTORS, atom_total), jnp.float32))
    tangent, image = lax.fori_loop(0, NEIGHBOURS, tangent_step, start)
    weighted = fsecond[None] * tangent

    def embed_step(slot_id, image):
        partner, direction, distance, parts = geometry(slot_id)
        return embed_update(image, direction, parts[1], amplitude[partner], amplitude, weighted, weighted[:, partner])
    image = lax.fori_loop(0, NEIGHBOURS, embed_step, image)
    count_all = 3.0 * atom_total
    gram = jnp.einsum('cka,cla->kl', vectors, vectors, precision=highest) / count_all
    mixed = jnp.einsum('cka,cla->kl', vectors, image, precision=highest) / count_all
    inverse, projected, right_side = project_block(gram, mixed)
    residual = jnp.einsum('cla,kl->cka', image, inverse, precision=highest) - jnp.einsum('cla,lk->cka', vectors, right_side, precision=highest)
    residual_rms = jnp.sqrt(lax.optimization_barrier(jnp.sum(residual * residual, axis=(0, 2))) / count_all + epsilon)
    return (residual.reshape((3 * VECTORS,) + lattice_shape), projected, residual_rms)
```

```python
import math

import jax
import jax.numpy as jnp
from jax import lax
from jax.experimental import pallas as pl
from jax.experimental.pallas import tpu as pltpu
from jax.sharding import PartitionSpec as P

lattice = 3.52
nearest = 3.52 / math.sqrt(2.0)
density_rate = 5.0
repulse_rate = 9.0
epsilon = 1e-06
vmem_bytes = 40 * 1024 * 1024

VEC = 32
CH = 3 * VEC
CHG = CH + 8
WCH = VEC + 8
LANES = 128
BITS = ((0, 0, 0), (1, 1, 0), (1, 0, 1), (0, 1, 1))


def directions():
    steps = []
    for p in range(3):
        for q in range(p + 1, 3):
            for a in (1, -1):
                for b in (1, -1):
                    step = [0, 0, 0]
                    step[p], step[q] = a, b
                    steps.append(tuple(step))
    for p in range(3):
        for a in (2, -2):
            step = [0, 0, 0]
            step[p] = a
            steps.append(tuple(step))
    return steps


STEPS = directions()
DIRS = len(STEPS)


def partner(sub, step):
    summed = [BITS[sub][c] + step[c] for c in range(3)]
    return BITS.index(tuple(v % 2 for v in summed)), tuple(v // 2 for v in summed)


def site_table():
    plain, shifted, table = [], [], {}
    for sub in range(4):
        for y in range(2):
            plain.append((0, 0, y, sub))
    for sub in range(4):
        for y in range(2):
            for d, step in enumerate(STEPS):
                other, off = partner(sub, step)
                key = (off[2], off[0], y + off[1], other)
                table[(sub, y, d)] = key
                base = (0,) + key[1:]
                if base not in plain:
                    plain.append(base)
                if key[0] != 0 and key not in shifted:
                    shifted.append(key)
    return plain, shifted, table


PLAIN, SHIFTED, TABLE = site_table()
ROWS = PLAIN + SHIFTED
INDEX = {key: i for i, key in enumerate(ROWS)}
UPPER = [key for key in SHIFTED if key[0] == 1]
LOWER = [key for key in SHIFTED if key[0] == -1]
Y_LOW, Y_HIGH = -1, 2


def table_rows():
    return jnp.asarray(
        [[INDEX[TABLE[(j // 2, j % 2, d)]] for d in range(DIRS)] for j in range(8)], jnp.int32
    )


def source(key, own, xm, xp, ym, yp, cm=None, cp=None):
    _, x, y, sub = key
    if x == 0 and 0 <= y < 2:
        return own, sub * 2 + y
    if x == 0:
        return (ym, sub) if y < 0 else (yp, sub)
    if 0 <= y < 2:
        return (xm if x < 0 else xp), sub * 2 + y
    side = cm if x < 0 else cp
    return side, 0 if y < 0 else 1


CORNER = {}
for _key in PLAIN:
    if _key[1] != 0 and not 0 <= _key[2] < 2:
        CORNER[(_key[1], _key[2])] = _key[3]


def call(kernel, outs, args, scratch=(), smem=(), name=None, cost=None):
    specs = [
        pl.BlockSpec(memory_space=pltpu.SMEM if i in smem else pltpu.VMEM) for i in range(len(args))
    ]
    return pl.pallas_call(
        kernel,
        out_shape=tuple(jax.ShapeDtypeStruct(s, jnp.float32) for s in outs),
        in_specs=specs,
        out_specs=tuple(pl.BlockSpec(memory_space=pltpu.VMEM) for _ in outs),
        scratch_shapes=list(scratch),
        compiler_params=pltpu.CompilerParams(vmem_limit_bytes=vmem_bytes),
        name=name,
    )(*args)


def own_rows_kernel(trial, shift, species, own, low, high):
    def step(j, carry):
        for c in range(3):
            own[j, c * VEC : (c + 1) * VEC, :] = trial[
                pl.ds(c * VEC * 8 + j, VEC, stride=8), :
            ]
        for c in range(3):
            own[j, CH + c : CH + c + 1, :] = shift[c, pl.ds(j, 1), :]
        own[j, CH + 3 : CH + 4, :] = species[pl.ds(j, 1), :].astype(jnp.float32)
        own[j, CH + 4 : CHG, :] = jnp.zeros((4, LANES), jnp.float32)
        return carry

    lax.fori_loop(0, 8, step, 0)
    for sub in range(4):
        low[sub] = own[sub * 2]
        high[sub] = own[sub * 2 + 1]


def edges_kernel(channels, own, xm, xp, ym, yp, to_low, to_high, to_xm, to_xp):
    lane = lax.broadcasted_iota(jnp.int32, (channels, LANES), 1)
    for keys, out, where in ((UPPER, to_low, 0), (LOWER, to_high, LANES - 1)):
        total = jnp.zeros((channels, LANES), jnp.float32)
        for i, key in enumerate(keys):
            ref, place = source(key, own, xm, xp, ym, yp)
            moved = pltpu.roll(ref[place], (i - where) % LANES, axis=1)
            total = jnp.where(lane == i, moved, total)
        out[...] = total
    for x, out in ((-1, to_xp), (1, to_xm)):
        out[0] = ym[CORNER[(x, Y_LOW)]]
        out[1] = yp[CORNER[(x, Y_HIGH)]]


def gather_rows(sites, channels, own, xm, xp, ym, yp, cm, cp, zm, zp):
    lane = lax.broadcasted_iota(jnp.int32, (channels, LANES), 1)
    for i, key in enumerate(PLAIN):
        ref, place = source(key, own, xm, xp, ym, yp, cm, cp)
        sites[i] = ref[place]
    for keys, columns, turn, edge in ((UPPER, zp, LANES - 1, LANES - 1), (LOWER, zm, 1, 0)):
        for i, key in enumerate(keys):
            ref, place = source((0,) + key[1:], own, xm, xp, ym, yp, cm, cp)
            moved = pltpu.roll(ref[place], turn, axis=1)
            column = pltpu.roll(columns[...], (edge - i) % LANES, axis=1)
            sites[INDEX[key]] = jnp.where(lane == edge, column, moved)


def site_params(species):
    alloy = (species == 1.0).astype(jnp.float32)
    return 0.1 - 0.03 * alloy, 3.0 - 0.8 * alloy, 0.35 - 0.05 * alloy


NCOEF = 13


def tangent_kernel(
    table, own, xm, xp, ym, yp, cm, cp, zm, zp, lists, counts,
    carried, low, high, coef, sites, geo, slope,
):
    gather_rows(sites, CHG, own, xm, xp, ym, yp, cm, cp, zm, zp)

    def place(j, carry):
        for d in range(DIRS):
            geo[pl.ds(d * 64 + j, 8, stride=8), :] = sites[table[j, d], CH:CHG, :]
        geo[pl.ds(DIRS * 64 + j, 8, stride=8), :] = own[j, CH:CHG, :]
        return carry

    lax.fori_loop(0, 8, place, 0)

    def quantity(d, n):
        return geo[d * 64 + n * 8 : d * 64 + n * 8 + 8, :]

    row = lax.broadcasted_iota(jnp.int32, (8, LANES), 0)
    lane = lax.broadcasted_iota(jnp.int32, (8, LANES), 1)
    sub, y = row // 2, row % 2
    live = counts[...]
    listed = [jnp.where(m < live, lists[m], -1) for m in range(lists.shape[0])]
    here = [quantity(DIRS, c) for c in range(3)]
    amp_here, embedding, pair_here = site_params(quantity(DIRS, 3))
    rho = jnp.zeros((8, LANES), jnp.float32)
    for d, step in enumerate(STEPS):
        amp, _, pair = site_params(quantity(d, 3))
        apart = [0.5 * lattice * step[c] + quantity(d, c) - here[c] for c in range(3)]
        distance = jnp.sqrt(apart[0] * apart[0] + apart[1] * apart[1] + apart[2] * apart[2])
        if 2 in step or -2 in step:
            off = [v // 2 for v in step]
            expected = ((sub * 3 + 1 + off[0]) * 4 + y + 1 + off[1]) * 130 + lane + 1 + off[2]
            found = listed[0] == expected
            for m in range(1, len(listed)):
                found = found | (listed[m] == expected)
            living = found.astype(jnp.float32)
        else:
            living = 1.0
        inverse = 1.0 / distance
        unit = [v * inverse for v in apart]
        scaled = distance / nearest - 1.0
        density = living * jnp.exp(-density_rate * scaled)
        dens1 = -(density_rate / nearest) * density
        dens2 = (density_rate / nearest) ** 2 * density
        potential = living * pair_here * pair * jnp.exp(-repulse_rate * scaled)
        pot1 = -(repulse_rate / nearest) * potential
        pot2 = (repulse_rate / nearest) ** 2 * potential
        rho = rho + amp * density
        both = amp * dens1
        values = unit + [both * v for v in unit]
        values += [
            pot2 - pot1 * inverse, dens2 - dens1 * inverse, pot1 * inverse, dens1 * inverse,
            both, amp_here * dens1, amp,
        ]
        for n, value in enumerate(values):
            coef[d * NCOEF + n] = value
    root = jnp.sqrt(rho)
    slope[0] = -embedding / (2.0 * root)
    slope[1] = embedding / (4.0 * rho * root)

    def tangents(j, carry):
        mine = [own[j, q * 8 : q * 8 + 8, :] for q in range(12)]
        total = [jnp.zeros((8, LANES), jnp.float32) for _ in range(4)]
        for d in range(DIRS):
            at = table[j, d]
            weight = [coef[d * NCOEF + 3 + c, pl.ds(j, 1), :] for c in range(3)]
            for k in range(4):
                for c in range(3):
                    q = c * 4 + k
                    total[k] = total[k] + weight[c] * (mine[q] - sites[at, q * 8 : q * 8 + 8, :])
        scale = slope[1, pl.ds(j, 1), :]
        for k in range(4):
            carried[j, k * 8 : k * 8 + 8, :] = total[k] * scale
        carried[j, VEC : VEC + 1, :] = slope[0, pl.ds(j, 1), :]
        carried[j, VEC + 1 : WCH, :] = jnp.zeros((WCH - VEC - 1, LANES), jnp.float32)
        return carry

    lax.fori_loop(0, 8, tangents, 0)
    for s in range(4):
        low[s] = carried[s * 2]
        high[s] = carried[s * 2 + 1]


def split(value):
    high = value.astype(jnp.bfloat16)
    return high, (value - high.astype(jnp.float32)).astype(jnp.bfloat16)


def image_kernel(
    table, own, xm, xp, ym, yp, cm, cp, zm, zp,
    w_own, w_xm, w_xp, w_ym, w_yp, w_cm, w_cp, w_zm, w_zp, coef,
    image, sums, sites, slopes, geo, mix,
):
    gather_rows(sites, CHG, own, xm, xp, ym, yp, cm, cp, zm, zp)
    gather_rows(slopes, WCH, w_own, w_xm, w_xp, w_ym, w_yp, w_cm, w_cp, w_zm, w_zp)

    def place(j, carry):
        for d in range(DIRS):
            geo[d, pl.ds(j, 1), :] = slopes[table[j, d], VEC : VEC + 1, :]
        geo[DIRS, pl.ds(j, 1), :] = w_own[j, VEC : VEC + 1, :]
        geo[DIRS + 1, pl.ds(j, 1), :] = own[j, CH + 3 : CH + 4, :]
        return carry

    lax.fori_loop(0, 8, place, 0)
    slope_here = geo[DIRS]
    amp_here, _, _ = site_params(geo[DIRS + 1])
    for d in range(DIRS):
        mixing = slope_here * coef[d * NCOEF + 12] + geo[d] * amp_here
        mix[d * 2] = coef[d * NCOEF + 6] + mixing * coef[d * NCOEF + 7]
        mix[d * 2 + 1] = coef[d * NCOEF + 8] + mixing * coef[d * NCOEF + 9]

    sums[...] = jnp.zeros_like(sums)

    def rows(j, carry):
        for half in range(2):
            kept = range(half * 2, half * 2 + 2)
            mine = {(c, k): own[j, (c * 4 + k) * 8 : (c * 4 + k) * 8 + 8, :] for c in range(3) for k in kept}
            bent = {k: w_own[j, k * 8 : k * 8 + 8, :] for k in kept}
            total = {q: jnp.zeros((8, LANES), jnp.float32) for q in mine}
            for d in range(DIRS):
                at = table[j, d]
                unit = [coef[d * NCOEF + c, pl.ds(j, 1), :] for c in range(3)]
                radial = mix[d * 2, pl.ds(j, 1), :]
                across = mix[d * 2 + 1, pl.ds(j, 1), :]
                there = coef[d * NCOEF + 10, pl.ds(j, 1), :]
                home = coef[d * NCOEF + 11, pl.ds(j, 1), :]
                for k in kept:
                    apart = [
                        mine[(c, k)] - sites[at, (c * 4 + k) * 8 : (c * 4 + k) * 8 + 8, :]
                        for c in range(3)
                    ]
                    along = unit[0] * apart[0] + unit[1] * apart[1] + unit[2] * apart[2]
                    push = radial * along + there * bent[k] + home * slopes[at, k * 8 : k * 8 + 8, :]
                    for c in range(3):
                        total[(c, k)] = total[(c, k)] + unit[c] * push + across * apart[c]
            for (c, k), value in total.items():
                image[j, (c * 4 + k) * 8 : (c * 4 + k) * 8 + 8, :] = value
        for c in range(3):
            high_v, low_v = split(own[j, c * VEC : (c + 1) * VEC, :])
            high_i, low_i = split(image[j, c * VEC : (c + 1) * VEC, :])
            right = jnp.concatenate([high_v, high_i], 0)
            left = jnp.concatenate([high_v, low_v, high_i, low_i], 0)
            sums[...] += lax.dot_general(
                left, right, (((1,), (1,)), ((), ())), preferred_element_type=jnp.float32
            )
        return carry

    lax.fori_loop(0, 8, rows, 0)


def factor(gram):
    row = lax.broadcasted_iota(jnp.int32, (VEC, VEC), 0)
    column = lax.broadcasted_iota(jnp.int32, (VEC, VEC), 1)
    work = jnp.concatenate([gram, (row == column).astype(jnp.float32)], 1)
    below = lax.broadcasted_iota(jnp.int32, (VEC, 2 * VEC), 0)
    for k in range(VEC - 1):
        top = work[k : k + 1, :]
        ratio = work[:, k : k + 1] * (1.0 / work[k : k + 1, k : k + 1])
        work = work - jnp.where(below > k, ratio * top, 0.0)
    pivots = jnp.sum(jnp.where(row == column, work[:, :VEC], 0.0), axis=1, keepdims=True)
    return work[:, VEC:] * (1.0 / jnp.sqrt(pivots))


def exact(a, b, dims):
    return lax.dot_general(
        a, b, (dims, ((), ())), precision=lax.Precision.HIGHEST, preferred_element_type=jnp.float32
    )


def residual_kernel(count_all, parts, own, image, residual, projected, squares):
    total = parts[0]
    for i in range(1, parts.shape[0]):
        total = total + parts[i]
    total = total / count_all
    gram, mixed = total[:VEC], total[VEC:]
    inverse = factor(gram)
    raw = exact(exact(inverse, mixed, ((1,), (0,))), inverse, ((1,), (1,)))
    other = exact(inverse, exact(inverse, mixed, ((1,), (0,))), ((1,), (1,)))
    sym = 0.5 * (raw + other)
    projected[...] = sym
    right = exact(sym, inverse, ((1,), (0,)))
    high, low = split(jnp.concatenate([inverse, -right], 1))
    left = jnp.concatenate([high, low, high], 1)
    squares[...] = jnp.zeros_like(squares)

    def rows(j, carry):
        for c in range(3):
            both = jnp.concatenate(
                [image[j, c * VEC : (c + 1) * VEC, :], own[j, c * VEC : (c + 1) * VEC, :]], 0
            )
            both_high, both_low = split(both)
            value = jnp.dot(
                left,
                jnp.concatenate([both_high, both_high, both_low], 0),
                preferred_element_type=jnp.float32,
            )
            residual[pl.ds(c * VEC * 8 + j, VEC, stride=8), :] = value
            squares[...] += value * value
        return carry

    lax.fori_loop(0, 8, rows, 0)


def shift(value, axis, by):
    peers = lax.axis_size(axis)
    return lax.ppermute(value, axis, [(i, (i + by) % peers) for i in range(peers)])


def gathered(value, axes):
    peers = 1
    for axis in axes:
        peers *= lax.axis_size(axis)
    return lax.all_to_all(
        jnp.broadcast_to(value[None], (peers,) + value.shape), axes, 0, 0, tiled=False
    )


def halo(channels, own, low, high):
    ym, yp = shift(high, "gy", 1), shift(low, "gy", -1)
    xm, xp = shift(own, "gx", 1), shift(own, "gx", -1)

    def kernel(*refs):
        edges_kernel(channels, *refs)

    column, pair = (channels, LANES), (2, channels, LANES)
    to_low, to_high, to_xm, to_xp = call(
        kernel, (column, column, pair, pair), (own, xm, xp, ym, yp), name="edges"
    )
    cm, cp = shift(to_xp, "gx", 1), shift(to_xm, "gx", -1)
    zm, zp = shift(to_high, "gz", 1), shift(to_low, "gz", -1)
    return xm, xp, ym, yp, cm, cp, zm, zp


def body(trial_block, site_shift, species, neighbours, counts):
    sizes = [lax.axis_size(axis) for axis in ("gx", "gy", "gz")]
    count_all = 3.0 * 1024 * sizes[0] * sizes[1] * sizes[2]
    table = table_rows()
    trial = trial_block.reshape(CH * 8, LANES)
    own, low, high = call(
        own_rows_kernel,
        ((8, CHG, LANES), (4, CHG, LANES), (4, CHG, LANES)),
        (trial, site_shift.reshape(3, 8, LANES), species.reshape(8, LANES)),
        name="own_rows",
    )
    around = halo(CHG, own, low, high)
    carried, low_w, high_w, coef = call(
        tangent_kernel,
        ((8, WCH, LANES), (4, WCH, LANES), (4, WCH, LANES), (DIRS * NCOEF, 8, LANES)),
        (table, own) + around + (neighbours.reshape(-1, 8, LANES), counts.reshape(8, LANES)),
        scratch=[
            pltpu.VMEM((len(ROWS), CHG, LANES), jnp.float32),
            pltpu.VMEM(((DIRS + 1) * 64, LANES), jnp.float32),
            pltpu.VMEM((2, 8, LANES), jnp.float32),
        ],
        smem=(0,),
        name="tangents",
    )
    around_w = halo(WCH, carried, low_w, high_w)
    image, sums = call(
        image_kernel,
        ((8, CH, LANES), (4 * VEC, 2 * VEC)),
        (table, own) + around + (carried,) + around_w + (coef,),
        scratch=[
            pltpu.VMEM((len(ROWS), CHG, LANES), jnp.float32),
            pltpu.VMEM((len(ROWS), WCH, LANES), jnp.float32),
            pltpu.VMEM((DIRS + 2, 8, LANES), jnp.float32),
            pltpu.VMEM((DIRS * 2, 8, LANES), jnp.float32),
        ],
        smem=(0,),
        name="images",
    )
    gram = sums[:VEC, :VEC] + sums[VEC : 2 * VEC, :VEC] + sums[VEC : 2 * VEC, :VEC].T
    mixed = (
        sums[:VEC, VEC:] + sums[VEC : 2 * VEC, VEC:] + sums[3 * VEC :, :VEC].T
    )
    local = jnp.concatenate([gram, mixed], 0)
    local = jnp.sum(gathered(local, ("gx", "gy")), 0)
    parts = gathered(local, ("gz",))

    def kernel(*refs):
        residual_kernel(count_all, *refs)

    residual, projected, squares = call(
        kernel,
        ((CH * 8, LANES), (VEC, VEC), (VEC, LANES)),
        (parts, own, image),
        name="residuals",
    )
    square = jnp.sum(squares, 1)
    square = jnp.sum(gathered(square, ("gx", "gy")), 0)
    square = jnp.sum(gathered(square, ("gz",)), 0) / count_all
    return residual.reshape(trial_block.shape), projected, jnp.sqrt(square + epsilon)


def solution(mesh):
    placed = (
        P(None, None, "gx", "gy", "gz"),
        P(None, None, "gx", "gy", "gz"),
        P(None, "gx", "gy", "gz"),
        P(None, None, "gx", "gy", "gz"),
        P(None, "gx", "gy", "gz"),
    )
    return jax.shard_map(
        body,
        mesh=mesh,
        in_specs=placed,
        out_specs=(P(None, None, "gx", "gy", "gz"), P(), P()),
        check_vma=False,
    )
```

```python
import math

import jax
import jax.numpy as jnp
from jax import lax
from jax.experimental import pallas as pl
from jax.experimental.pallas import tpu as pltpu
from jax.sharding import PartitionSpec as P

lattice = 3.52
nearest = 3.52 / math.sqrt(2.0)
density_rate = 5.0
repulse_rate = 9.0
epsilon = 1e-06
vmem_bytes = 40 * 1024 * 1024

VEC = 32
CH = 3 * VEC
CHG = CH + 8
WCH = VEC + 8
LANES = 128
BITS = ((0, 0, 0), (1, 1, 0), (1, 0, 1), (0, 1, 1))


def directions():
    steps = []
    for p in range(3):
        for q in range(p + 1, 3):
            for a in (1, -1):
                for b in (1, -1):
                    step = [0, 0, 0]
                    step[p], step[q] = a, b
                    steps.append(tuple(step))
    for p in range(3):
        for a in (2, -2):
            step = [0, 0, 0]
            step[p] = a
            steps.append(tuple(step))
    return steps


STEPS = directions()
DIRS = len(STEPS)
NEAR = 12


def partner(sub, step):
    summed = [BITS[sub][c] + step[c] for c in range(3)]
    return BITS.index(tuple(v % 2 for v in summed)), tuple(v // 2 for v in summed)


def site_table():
    plain, shifted, table = [], [], {}
    for sub in range(4):
        for y in range(2):
            plain.append((0, 0, y, sub))
    for sub in range(4):
        for y in range(2):
            for d, step in enumerate(STEPS):
                other, off = partner(sub, step)
                key = (off[2], off[0], y + off[1], other)
                table[(sub, y, d)] = key
                base = (0,) + key[1:]
                if base not in plain:
                    plain.append(base)
                if key[0] != 0 and key not in shifted:
                    shifted.append(key)
    return plain, shifted, table


PLAIN, SHIFTED, TABLE = site_table()
ROWS = PLAIN + SHIFTED
INDEX = {key: i for i, key in enumerate(ROWS)}
Y_LOW, Y_HIGH = -1, 2


def bring_kernel(own_in, alive_in, after, own, alive):
    own[...] = own_in[...]
    alive[...] = alive_in[...]


def fill_table(table):
    for j in range(8):
        for d in range(DIRS):
            table[j, d] = INDEX[TABLE[(j // 2, j % 2, d)]]


def source(key, channels, own, xm, xp, ym, yp, cm, cp):
    _, x, y, sub = key
    if x == 0 and 0 <= y < 2:
        return own[sub * 2 + y]
    if x == 0:
        return (ym if y < 0 else yp)[sub * channels : (sub + 1) * channels, :]
    if 0 <= y < 2:
        return (xm if x < 0 else xp)[sub * 2 + y]
    place = 0 if x < 0 else channels
    return (cm if y < 0 else cp)[place : place + channels, :]


def column_of(key):
    sz, x, y, sub = key
    group = {(-1, 0): 1, (1, 0): 2, (0, -1): 3, (0, 1): 4, (0, 0): 0}[
        (x, 0 if 0 <= y < 2 else (-1 if y < 0 else 1))
    ]
    return group * 16 + (0 if sz == 1 else 8) + sub * 2 + y % 2


CORNER = {}
for _key in PLAIN:
    if _key[1] != 0 and not 0 <= _key[2] < 2:
        CORNER[(_key[1], _key[2])] = _key[3]


def call(kernel, outs, args, scratch=(), hbm=(), hbm_outs=(), smem_outs=(), name=None, limit=vmem_bytes):
    outs = [s + (jnp.float32,) if isinstance(s[-1], int) else s for s in outs]
    spaces = [
        pltpu.HBM if i in hbm_outs else pltpu.SMEM if i in smem_outs else pltpu.VMEM
        for i in range(len(outs))
    ]
    return pl.pallas_call(
        kernel,
        out_shape=tuple(jax.ShapeDtypeStruct(s[:-1], s[-1]) for s in outs),
        in_specs=[
            pl.BlockSpec(memory_space=pltpu.HBM if i in hbm else pltpu.VMEM)
            for i in range(len(args))
        ],
        out_specs=tuple(pl.BlockSpec(memory_space=space) for space in spaces),
        scratch_shapes=list(scratch),
        compiler_params=pltpu.CompilerParams(vmem_limit_bytes=limit),
        name=name,
    )(*args)


def own_rows_kernel(
    trial_hbm, shift_hbm, species_hbm, lists_hbm, counts_hbm,
    own, low, high, columns, alive, trial, shift, species, lists, counts, sems,
):
    copies = [
        pltpu.make_async_copy(shift_hbm, shift, sems.at[0]),
        pltpu.make_async_copy(species_hbm, species, sems.at[1]),
    ]
    for c in range(3):
        part = pl.ds(c * VEC * 8, VEC * 8)
        copies.append(pltpu.make_async_copy(trial_hbm.at[part], trial.at[part], sems.at[2 + c]))
    copies.append(pltpu.make_async_copy(lists_hbm, lists, sems.at[5]))
    copies.append(pltpu.make_async_copy(counts_hbm, counts, sems.at[6]))
    for copy in copies:
        copy.start()

    def small(j, carry):
        for c in range(3):
            own[j, CH + c : CH + c + 1, :] = shift[c, pl.ds(j, 1), :]
        own[j, CH + 3 : CH + 4, :] = species[pl.ds(j, 1), :].astype(jnp.float32)
        own[j, CH + 4 : CHG, :] = jnp.zeros((4, LANES), jnp.float32)
        return carry

    copies[0].wait()
    copies[1].wait()
    lax.fori_loop(0, 8, small, 0)
    for c in range(3):

        def large(j, carry):
            own[j, c * VEC : (c + 1) * VEC, :] = trial[pl.ds(c * VEC * 8 + j, VEC, stride=8), :]
            return carry

        copies[2 + c].wait()
        lax.fori_loop(0, 8, large, 0)
    for sub in range(4):
        low[sub * CHG : (sub + 1) * CHG, :] = own[sub * 2]
        high[sub * CHG : (sub + 1) * CHG, :] = own[sub * 2 + 1]
    columns[...] = edge_columns(CHG, own)
    copies[5].wait()
    copies[6].wait()
    row = lax.broadcasted_iota(jnp.int32, (8, LANES), 0)
    lane = lax.broadcasted_iota(jnp.int32, (8, LANES), 1)
    sub, y = row // 2, row % 2
    live = counts[...]
    listed = [jnp.where(m < live, lists[m], -1) for m in range(lists.shape[0])]
    for i, step in enumerate(STEPS[NEAR:]):
        off = [v // 2 for v in step]
        expected = ((sub * 3 + 1 + off[0]) * 4 + y + 1 + off[1]) * 130 + lane + 1 + off[2]
        found = listed[0] == expected
        for m in range(1, len(listed)):
            found = found | (listed[m] == expected)
        alive[i] = found.astype(jnp.float32)


def edge_columns(channels, own):
    lane = lax.broadcasted_iota(jnp.int32, (channels, LANES), 1)
    total = jnp.zeros((channels, LANES), jnp.float32)
    for j in range(8):
        row = own[j]
        total = jnp.where(lane == j, pltpu.roll(row, j, axis=1) if j else row, total)
        total = jnp.where(lane == 8 + j, pltpu.roll(row, 9 + j, axis=1), total)
    full = jnp.concatenate([total, jnp.zeros((LANES - channels, LANES), jnp.float32)], 0)
    return full.T[:16]


def gather_rows(sites, channels, own, xm, xp, ym, yp, cm, cp, xcm, xcp, zc):
    lane = lax.broadcasted_iota(jnp.int32, (channels, LANES), 1)
    for i, key in enumerate(PLAIN):
        sites[i] = source(key, channels, own, xm, xp, ym, yp, cm, cp)
    groups = [zc[...], xcm[...], xcp[...]] + [ref[2 * channels :, :] for ref in (cm, cp)]
    groups.append(jnp.zeros((LANES - 80, LANES), jnp.float32))
    columns = jnp.concatenate(groups, 0).T[:channels]
    for key in SHIFTED:
        turn, edge = (LANES - 1, LANES - 1) if key[0] == 1 else (1, 0)
        moved = pltpu.roll(sites[INDEX[(0,) + key[1:]]], turn, axis=1)
        by = (edge - column_of(key)) % LANES
        column = pltpu.roll(columns, by, axis=1) if by else columns
        sites[INDEX[key]] = jnp.where(lane == edge, column, moved)


def site_params(species):
    alloy = (species == 1.0).astype(jnp.float32)
    return 0.1 - 0.03 * alloy, 3.0 - 0.8 * alloy, 0.35 - 0.05 * alloy


NCOEF = 13


def tangent_kernel(
    own, xm, xp, ym, yp, cm, cp, xcm, xcp, zc, alive,
    carried, low, high, columns, coef, sites, table, geo, slope,
):
    fill_table(table)
    gather_rows(sites, CHG, own, xm, xp, ym, yp, cm, cp, xcm, xcp, zc)

    def place(j, carry):
        for d in range(DIRS):
            geo[pl.ds(d * 64 + j, 8, stride=8), :] = sites[table[j, d], CH:CHG, :]
        geo[pl.ds(DIRS * 64 + j, 8, stride=8), :] = own[j, CH:CHG, :]
        return carry

    lax.fori_loop(0, 8, place, 0)

    def quantity(d, n):
        return geo[d * 64 + n * 8 : d * 64 + n * 8 + 8, :]

    here = [quantity(DIRS, c) for c in range(3)]
    amp_here, embedding, pair_here = site_params(quantity(DIRS, 3))
    rho = jnp.zeros((8, LANES), jnp.float32)
    for d, step in enumerate(STEPS):
        amp, _, pair = site_params(quantity(d, 3))
        apart = [0.5 * lattice * step[c] + quantity(d, c) - here[c] for c in range(3)]
        distance = jnp.sqrt(apart[0] * apart[0] + apart[1] * apart[1] + apart[2] * apart[2])
        living = alive[d - NEAR] if d >= NEAR else 1.0
        inverse = 1.0 / distance
        unit = [v * inverse for v in apart]
        scaled = distance / nearest - 1.0
        density = living * jnp.exp(-density_rate * scaled)
        dens1 = -(density_rate / nearest) * density
        dens2 = (density_rate / nearest) ** 2 * density
        potential = living * pair_here * pair * jnp.exp(-repulse_rate * scaled)
        pot1 = -(repulse_rate / nearest) * potential
        pot2 = (repulse_rate / nearest) ** 2 * potential
        rho = rho + amp * density
        both = amp * dens1
        values = unit + [both * v for v in unit]
        values += [
            pot2 - pot1 * inverse, dens2 - dens1 * inverse, pot1 * inverse, dens1 * inverse,
            both, amp_here * dens1, amp,
        ]
        for n, value in enumerate(values):
            coef[d * NCOEF + n] = value
    root = jnp.sqrt(rho)
    slope[0] = -embedding / (2.0 * root)
    slope[1] = embedding / (4.0 * rho * root)

    def tangents(j, carry):
        mine = [own[j, q * 8 : q * 8 + 8, :] for q in range(12)]
        total = [jnp.zeros((8, LANES), jnp.float32) for _ in range(4)]
        for d in range(DIRS):
            at = table[j, d]
            weight = [coef[d * NCOEF + 3 + c, pl.ds(j, 1), :] for c in range(3)]
            for k in range(4):
                for c in range(3):
                    q = c * 4 + k
                    total[k] = total[k] + weight[c] * (mine[q] - sites[at, q * 8 : q * 8 + 8, :])
        scale = slope[1, pl.ds(j, 1), :]
        for k in range(4):
            carried[j, k * 8 : k * 8 + 8, :] = total[k] * scale
        carried[j, VEC : VEC + 1, :] = slope[0, pl.ds(j, 1), :]
        carried[j, VEC + 1 : WCH, :] = jnp.zeros((WCH - VEC - 1, LANES), jnp.float32)
        return carry

    lax.fori_loop(0, 8, tangents, 0)
    for s in range(4):
        low[s * WCH : (s + 1) * WCH, :] = carried[s * 2]
        high[s * WCH : (s + 1) * WCH, :] = carried[s * 2 + 1]
    columns[...] = edge_columns(WCH, carried)


def split(value):
    high = value.astype(jnp.bfloat16)
    return high, (value - high.astype(jnp.float32)).astype(jnp.bfloat16)


def mask_iota():
    row = lax.broadcasted_iota(jnp.int32, (VEC, VEC), 0)
    column = lax.broadcasted_iota(jnp.int32, (VEC, VEC), 1)
    return row, column


def packed(gram, mixed, energy):
    row, column = mask_iota()
    first = jnp.where(row <= column, gram, energy)
    even = 0.5 * (mixed + mixed.T)
    diagonal = jnp.sum(jnp.where(row == column, energy, 0.0), axis=1, keepdims=True)
    second = jnp.where(row <= column, even, jnp.where(row == column + 1, diagonal, 0.0))
    corner = jnp.broadcast_to(diagonal[0:1, :], (VEC, VEC))
    second = jnp.where((row == VEC - 1) & (column == 0), corner, second)
    half = VEC // 2
    return jnp.concatenate([first[:half], second[:half], first[half:], second[half:]], 1)


def unpacked(block):
    row, column = mask_iota()
    first = jnp.concatenate([block[:, :VEC], block[:, 2 * VEC : 3 * VEC]], 0)
    second = jnp.concatenate([block[:, VEC : 2 * VEC], block[:, 3 * VEC :]], 0)
    diagonal = jnp.sum(jnp.where(row == column + 1, second, 0.0), axis=1, keepdims=True)
    corner = jnp.broadcast_to(second[VEC - 1 :, 0:1], (VEC, 1))
    diagonal = jnp.where(row[:, 0:1] == 0, corner, diagonal)
    gram = jnp.where(row <= column, first, first.T)
    mixed = jnp.where(row <= column, second, second.T)
    energy = jnp.where(row == column, diagonal, jnp.where(row > column, first, first.T))
    return gram, mixed, energy


def image_kernel(
    own, sites, coef, w_own, w_xm, w_xp, w_ym, w_yp, w_cm, w_cp, w_xcm, w_xcp, w_zc,
    local, pieces, table, image, slopes, geo, mix, sums,
):
    fill_table(table)
    gather_rows(slopes, WCH, w_own, w_xm, w_xp, w_ym, w_yp, w_cm, w_cp, w_xcm, w_xcp, w_zc)

    def place(j, carry):
        for d in range(DIRS):
            geo[d, pl.ds(j, 1), :] = slopes[table[j, d], VEC : VEC + 1, :]
        geo[DIRS, pl.ds(j, 1), :] = w_own[j, VEC : VEC + 1, :]
        geo[DIRS + 1, pl.ds(j, 1), :] = own[j, CH + 3 : CH + 4, :]
        return carry

    lax.fori_loop(0, 8, place, 0)
    slope_here = geo[DIRS]
    amp_here, _, _ = site_params(geo[DIRS + 1])
    lean = [jnp.zeros((8, LANES), jnp.float32) for _ in range(3)]
    for d in range(DIRS):
        mixing = slope_here * coef[d * NCOEF + 12] + geo[d] * amp_here
        mix[d * 2] = coef[d * NCOEF + 6] + mixing * coef[d * NCOEF + 7]
        mix[d * 2 + 1] = coef[d * NCOEF + 8] + mixing * coef[d * NCOEF + 9]
        lean = [lean[c] + coef[d * NCOEF + c] * coef[d * NCOEF + 10] for c in range(3)]
    for c in range(3):
        geo[c] = lean[c]

    sums[...] = jnp.zeros_like(sums)
    blocks = [(c, k) for c in range(3) for k in range(4)]

    def rows(j, carry):
        mine = {b: own[j, (b[0] * 4 + b[1]) * 8 : (b[0] * 4 + b[1]) * 8 + 8, :] for b in blocks}
        total = {}
        for c in range(3):
            leaning = geo[c, pl.ds(j, 1), :]
            for k in range(4):
                total[(c, k)] = leaning * w_own[j, k * 8 : k * 8 + 8, :]
        for d in range(DIRS):
            at = table[j, d]
            unit = [coef[d * NCOEF + c, pl.ds(j, 1), :] for c in range(3)]
            radial = mix[d * 2, pl.ds(j, 1), :]
            across = mix[d * 2 + 1, pl.ds(j, 1), :]
            home = coef[d * NCOEF + 11, pl.ds(j, 1), :]
            for k in range(4):
                apart = [
                    mine[(c, k)] - sites[at, (c * 4 + k) * 8 : (c * 4 + k) * 8 + 8, :]
                    for c in range(3)
                ]
                along = unit[0] * apart[0] + unit[1] * apart[1] + unit[2] * apart[2]
                push = radial * along + home * slopes[at, k * 8 : k * 8 + 8, :]
                for c in range(3):
                    total[(c, k)] = total[(c, k)] + unit[c] * push + across * apart[c]
        for (c, k), value in total.items():
            image[(c * 4 + k) * 8 : (c * 4 + k) * 8 + 8, :] = value
        wide = []
        for c in range(3):
            both = jnp.concatenate(
                [image[c * VEC : (c + 1) * VEC, :], own[j, c * VEC : (c + 1) * VEC, :]], 0
            )
            wide.append(jnp.concatenate(split(both), 0))
        wide = jnp.concatenate(wide, 1)
        pieces[j] = wide
        sums[...] += lax.dot_general(
            wide, wide, (((1,), (1,)), ((), ())), preferred_element_type=jnp.float32
        )
        return carry

    lax.fori_loop(0, 8, rows, 0)
    whole = sums[...]
    folded = whole[: 2 * VEC] + whole[2 * VEC :]
    folded = folded[:, : 2 * VEC] + folded[:, 2 * VEC :]
    block = packed(folded[VEC:, VEC:], folded[VEC:, :VEC], folded[:VEC, :VEC])
    for i in range(local.shape[0]):
        local[i] = block


def add_kernel(parts, out):
    total = parts[0]
    for i in range(1, parts.shape[0]):
        total = total + parts[i]
    for i in range(out.shape[0]):
        out[i] = total


def factor(gram):
    row, column = mask_iota()
    work = jnp.concatenate([gram, (row == column).astype(jnp.float32)], 1)
    below = lax.broadcasted_iota(jnp.int32, (VEC, 2 * VEC), 0)
    for k in range(VEC - 1):
        top = work[k : k + 1, :]
        ratio = work[:, k : k + 1] * (1.0 / work[k : k + 1, k : k + 1])
        work = work - jnp.where(below > k, ratio * top, 0.0)
    pivots = jnp.sum(jnp.where(row == column, work[:, :VEC], 0.0), axis=1, keepdims=True)
    return work[:, VEC:] * (1.0 / jnp.sqrt(pivots))


def exact(a, b, dims):
    return lax.dot_general(
        a, b, (dims, ((), ())), precision=lax.Precision.HIGHEST, preferred_element_type=jnp.float32
    )


def residual_kernel(
    count_all, parts, pieces, residual_hbm, projected, rms, lost, here, residual, squares, sems
):
    total = parts[0]
    for i in range(1, parts.shape[0]):
        total = total + parts[i]
    gram, mixed, energy = unpacked(total / count_all)
    inverse = factor(gram)
    turned = exact(inverse, jnp.concatenate([mixed, energy], 1), ((1,), (0,)))
    raw = exact(turned[:, :VEC], inverse, ((1,), (1,)))
    sym = 0.5 * (raw + raw.T)
    projected[...] = sym
    right = exact(sym, inverse, ((1,), (0,)))
    high, low = split(jnp.concatenate([inverse, -right], 1))
    left = jnp.concatenate([high, high, low], 1)
    squares[...] = jnp.zeros_like(squares)
    for j in range(8):
        value = jnp.dot(
            left,
            jnp.concatenate([pieces[j], pieces[j, : 2 * VEC]], 0),
            preferred_element_type=jnp.float32,
        )
        for c in range(3):
            part = value[:, c * LANES : (c + 1) * LANES]
            residual[pl.ds(c * VEC * 8 + j, VEC, stride=8), :] = part
            squares[...] += part * part
    copy = pltpu.make_async_copy(residual, residual_hbm, sems.at[0])
    copy.start()
    norms = jnp.sum(turned[:, VEC:] * inverse, axis=1, keepdims=True)
    left_over = norms - jnp.sum(sym * sym, axis=1, keepdims=True)
    wide = jnp.concatenate(
        [
            jnp.broadcast_to(jnp.sqrt(left_over + epsilon), (VEC, LANES)),
            jnp.broadcast_to(jnp.sum(squares[...], axis=1, keepdims=True), (VEC, LANES)),
            jnp.zeros((LANES - 2 * VEC, LANES), jnp.float32),
        ],
        0,
    ).T
    rms[...] = wide[0:1, :VEC]
    here[...] = wide[0:1, VEC : 2 * VEC]
    kept = jnp.where(left_over > 0.02 * norms, 0, 1)
    lost[0, 0] = jnp.max(kept)
    copy.wait()


def shift(value, axis, by):
    axis = ("ga", "gb") if axis == "gy" else axis
    peers = peers_of(axis) if isinstance(axis, tuple) else lax.axis_size(axis)
    return lax.ppermute(value, axis, [(i, (i + by) % peers) for i in range(peers)])


def exchanged(parts, axes):
    return lax.all_to_all(parts, axes, 0, 0, tiled=False)


def halo(channels, own, low, high, columns):
    ym, yp = shift(high, "gy", 1), shift(low, "gy", -1)
    zm, zp = shift(columns, "gz", 1), shift(columns, "gz", -1)
    xm, xp = shift(own, "gx", 1), shift(own, "gx", -1)
    row = lax.broadcasted_iota(jnp.int32, columns.shape, 0)
    zc = jnp.where(row < 8, zp, zm)

    def corners(side, y):
        rows = [(xm, CORNER[(-1, side)] * 2 + y), (xp, CORNER[(1, side)] * 2 + y)]
        return jnp.concatenate([face[j] for face, j in rows] + [zc], 0)

    cm, cp = shift(corners(Y_LOW, 1), "gy", 1), shift(corners(Y_HIGH, 0), "gy", -1)
    xcm, xcp = shift(zc, "gx", 1), shift(zc, "gx", -1)
    return xm, xp, ym, yp, cm, cp, xcm, xcp, zc


FIRST, SECOND = ("gx", "gb"), ("ga", "gz")


def peers_of(axes):
    return math.prod(lax.axis_size(axis) for axis in axes)


def body(trial_block, site_shift, species, neighbours, counts):
    first, second = peers_of(FIRST), peers_of(SECOND)
    count_all = 3.0 * 1024 * first * second
    vmem = lambda shape, dtype=jnp.float32: pltpu.VMEM(shape, dtype)
    lists = neighbours.reshape(-1, 8, LANES)
    edge = (16, LANES)
    table = pltpu.SMEM((8, DIRS), jnp.int32)
    own, low, high, columns, alive = call(
        own_rows_kernel,
        ((8, CHG, LANES), (4 * CHG, LANES), (4 * CHG, LANES), edge, (DIRS - NEAR, 8, LANES)),
        (
            trial_block.reshape(CH * 8, LANES),
            site_shift.reshape(3, 8, LANES),
            species.reshape(8, LANES),
            lists,
            counts.reshape(8, LANES),
        ),
        scratch=[
            vmem((CH * 8, LANES)), vmem((3, 8, LANES)), vmem((8, LANES), jnp.int32),
            vmem(lists.shape, jnp.int32), vmem((8, LANES), jnp.int32),
            pltpu.SemaphoreType.DMA((7,)),
        ],
        hbm=(0, 1, 2, 3, 4),
        name="own_rows",
        limit=60 * 1024 * 1024,
    )
    around = halo(CHG, own, low, high, columns)
    own, alive = call(
        bring_kernel, (own.shape, alive.shape), (own, alive, around[-1]), name="bring"
    )
    carried, low_w, high_w, columns_w, coef, sites = call(
        tangent_kernel,
        (
            (8, WCH, LANES), (4 * WCH, LANES), (4 * WCH, LANES), edge, (DIRS * NCOEF, 8, LANES),
            (len(ROWS), CHG, LANES),
        ),
        (own,) + around + (alive,),
        scratch=[table, vmem(((DIRS + 1) * 64, LANES)), vmem((2, 8, LANES))],
        name="tangents",
    )
    around_w = halo(WCH, carried, low_w, high_w, columns_w)
    local, pieces = call(
        image_kernel,
        ((first, VEC // 2, LANES), (8, 4 * VEC, 3 * LANES, jnp.bfloat16)),
        (own, sites, coef, carried) + around_w,
        scratch=[
            table, vmem((CH, LANES)), vmem((len(ROWS), WCH, LANES)),
            vmem((DIRS + 2, 8, LANES)), vmem((DIRS * 2, 8, LANES)), vmem((4 * VEC, 4 * VEC)),
        ],
        name="images",
    )
    (group,) = call(
        add_kernel, ((second, VEC // 2, LANES),), (exchanged(local, FIRST),), name="group_sum"
    )

    def kernel(*refs):
        residual_kernel(count_all, *refs)

    residual, projected, rms, lost, here = call(
        kernel,
        ((CH * 8, LANES), (VEC, VEC), (1, VEC), (1, 1, jnp.int32), (1, VEC)),
        (exchanged(group, SECOND), pieces),
        scratch=[vmem((CH * 8, LANES)), vmem((VEC, LANES)), pltpu.SemaphoreType.DMA((1,))],
        hbm_outs=(0,),
        smem_outs=(3,),
        name="residuals",
    )
    rms = lax.cond(
        lost[0, 0] != 0,
        lambda: jnp.sqrt(lax.psum(here, FIRST + SECOND) / count_all + epsilon),
        lambda: rms,
    )
    return residual.reshape(trial_block.shape), projected, rms.reshape(VEC)


def solution(mesh):
    grid = mesh.devices
    halves = jax.sharding.Mesh(
        grid.reshape(grid.shape[0], 2, grid.shape[1] // 2, grid.shape[2]), ("gx", "ga", "gb", "gz")
    )
    cells = ("gx", ("ga", "gb"), "gz")
    placed = (
        P(None, None, *cells),
        P(None, None, *cells),
        P(None, *cells),
        P(None, None, *cells),
        P(None, *cells),
    )
    return jax.shard_map(
        body,
        mesh=halves,
        in_specs=placed,
        out_specs=(P(None, None, *cells), P(), P()),
        check_vma=False,
    )
```

```python
import math

import jax
import jax.numpy as jnp
from jax import lax
from jax.experimental import pallas as pl
from jax.experimental.pallas import tpu as pltpu
from jax.sharding import PartitionSpec as P

lattice = 3.52
nearest = 3.52 / math.sqrt(2.0)
density_rate = 5.0
repulse_rate = 9.0
epsilon = 1e-06
vmem_bytes = 40 * 1024 * 1024

VEC = 32
CH = 3 * VEC
CHG = CH + 8
WCH = VEC + 8
LANES = 128
BITS = ((0, 0, 0), (1, 1, 0), (1, 0, 1), (0, 1, 1))


def directions():
    steps = []
    for p in range(3):
        for q in range(p + 1, 3):
            for a in (1, -1):
                for b in (1, -1):
                    step = [0, 0, 0]
                    step[p], step[q] = a, b
                    steps.append(tuple(step))
    for p in range(3):
        for a in (2, -2):
            step = [0, 0, 0]
            step[p] = a
            steps.append(tuple(step))
    return steps


STEPS = directions()
DIRS = len(STEPS)
NEAR = 12


def partner(sub, step):
    summed = [BITS[sub][c] + step[c] for c in range(3)]
    return BITS.index(tuple(v % 2 for v in summed)), tuple(v // 2 for v in summed)


def site_table():
    plain, shifted, table = [], [], {}
    for sub in range(4):
        for y in range(2):
            plain.append((0, 0, y, sub))
    for sub in range(4):
        for y in range(2):
            for d, step in enumerate(STEPS):
                other, off = partner(sub, step)
                key = (off[2], off[0], y + off[1], other)
                table[(sub, y, d)] = key
                base = (0,) + key[1:]
                if base not in plain:
                    plain.append(base)
                if key[0] != 0 and key not in shifted:
                    shifted.append(key)
    return plain, shifted, table


PLAIN, SHIFTED, TABLE = site_table()
ROWS = PLAIN + SHIFTED
INDEX = {key: i for i, key in enumerate(ROWS)}
Y_LOW, Y_HIGH = -1, 2


def bring_kernel(own_in, alive_in, after, own, alive):
    own[...] = own_in[...]
    alive[...] = alive_in[...]


def fill_table(table):
    for j in range(8):
        for d in range(DIRS):
            table[j, d] = INDEX[TABLE[(j // 2, j % 2, d)]]


def source(key, channels, own, xm, xp, ym, yp, cm, cp):
    _, x, y, sub = key
    if x == 0 and 0 <= y < 2:
        return own[sub * 2 + y]
    if x == 0:
        return (ym if y < 0 else yp)[sub * channels : (sub + 1) * channels, :]
    if 0 <= y < 2:
        return (xm if x < 0 else xp)[sub * 2 + y]
    place = 0 if x < 0 else channels
    return (cm if y < 0 else cp)[place : place + channels, :]


def column_of(key):
    sz, x, y, sub = key
    group = {(-1, 0): 1, (1, 0): 2, (0, -1): 3, (0, 1): 4, (0, 0): 0}[
        (x, 0 if 0 <= y < 2 else (-1 if y < 0 else 1))
    ]
    return group * 16 + (0 if sz == 1 else 8) + sub * 2 + y % 2


CORNER = {}
for _key in PLAIN:
    if _key[1] != 0 and not 0 <= _key[2] < 2:
        CORNER[(_key[1], _key[2])] = _key[3]


def call(kernel, outs, args, scratch=(), hbm=(), hbm_outs=(), smem_outs=(), name=None, limit=vmem_bytes):
    outs = [s + (jnp.float32,) if isinstance(s[-1], int) else s for s in outs]
    spaces = [
        pltpu.HBM if i in hbm_outs else pltpu.SMEM if i in smem_outs else pltpu.VMEM
        for i in range(len(outs))
    ]
    return pl.pallas_call(
        kernel,
        out_shape=tuple(jax.ShapeDtypeStruct(s[:-1], s[-1]) for s in outs),
        in_specs=[
            pl.BlockSpec(memory_space=pltpu.HBM if i in hbm else pltpu.VMEM)
            for i in range(len(args))
        ],
        out_specs=tuple(pl.BlockSpec(memory_space=space) for space in spaces),
        scratch_shapes=list(scratch),
        compiler_params=pltpu.CompilerParams(vmem_limit_bytes=limit),
        name=name,
    )(*args)


def own_rows_kernel(
    trial_hbm, shift_hbm, species_hbm, lists_hbm, counts_hbm,
    own, low, high, columns, alive, trial, shift, species, lists, counts, sems,
):
    copies = [
        pltpu.make_async_copy(shift_hbm, shift, sems.at[0]),
        pltpu.make_async_copy(species_hbm, species, sems.at[1]),
    ]
    for c in range(3):
        part = pl.ds(c * VEC * 8, VEC * 8)
        copies.append(pltpu.make_async_copy(trial_hbm.at[part], trial.at[part], sems.at[2 + c]))
    copies.append(pltpu.make_async_copy(lists_hbm, lists, sems.at[5]))
    copies.append(pltpu.make_async_copy(counts_hbm, counts, sems.at[6]))
    for copy in copies:
        copy.start()

    def small(j, carry):
        for c in range(3):
            own[j, CH + c : CH + c + 1, :] = shift[c, pl.ds(j, 1), :]
        own[j, CH + 3 : CH + 4, :] = species[pl.ds(j, 1), :].astype(jnp.float32)
        own[j, CH + 4 : CHG, :] = jnp.zeros((4, LANES), jnp.float32)
        return carry

    copies[0].wait()
    copies[1].wait()
    lax.fori_loop(0, 8, small, 0)
    for c in range(3):

        def large(j, carry):
            own[j, c * VEC : (c + 1) * VEC, :] = trial[pl.ds(c * VEC * 8 + j, VEC, stride=8), :]
            return carry

        copies[2 + c].wait()
        lax.fori_loop(0, 8, large, 0)
    for sub in range(4):
        low[sub * CHG : (sub + 1) * CHG, :] = own[sub * 2]
        high[sub * CHG : (sub + 1) * CHG, :] = own[sub * 2 + 1]
    columns[...] = edge_columns(CHG, own)
    copies[5].wait()
    copies[6].wait()
    row = lax.broadcasted_iota(jnp.int32, (8, LANES), 0)
    lane = lax.broadcasted_iota(jnp.int32, (8, LANES), 1)
    sub, y = row // 2, row % 2
    live = counts[...]
    listed = [jnp.where(m < live, lists[m], -1) for m in range(lists.shape[0])]
    for i, step in enumerate(STEPS[NEAR:]):
        off = [v // 2 for v in step]
        expected = ((sub * 3 + 1 + off[0]) * 4 + y + 1 + off[1]) * 130 + lane + 1 + off[2]
        found = listed[0] == expected
        for m in range(1, len(listed)):
            found = found | (listed[m] == expected)
        alive[i] = found.astype(jnp.float32)


def edge_columns(channels, own):
    lane = lax.broadcasted_iota(jnp.int32, (channels, LANES), 1)
    total = jnp.zeros((channels, LANES), jnp.float32)
    for j in range(8):
        row = own[j]
        total = jnp.where(lane == j, pltpu.roll(row, j, axis=1) if j else row, total)
        total = jnp.where(lane == 8 + j, pltpu.roll(row, 9 + j, axis=1), total)
    full = jnp.concatenate([total, jnp.zeros((LANES - channels, LANES), jnp.float32)], 0)
    return full.T[:16]


def gather_rows(sites, channels, own, xm, xp, ym, yp, cm, cp, xcm, xcp, zc):
    lane = lax.broadcasted_iota(jnp.int32, (channels, LANES), 1)
    for i, key in enumerate(PLAIN):
        sites[i] = source(key, channels, own, xm, xp, ym, yp, cm, cp)
    groups = [zc[...], xcm[...], xcp[...]] + [ref[2 * channels :, :] for ref in (cm, cp)]
    groups.append(jnp.zeros((LANES - 80, LANES), jnp.float32))
    columns = jnp.concatenate(groups, 0).T[:channels]
    for key in SHIFTED:
        turn, edge = (LANES - 1, LANES - 1) if key[0] == 1 else (1, 0)
        moved = pltpu.roll(sites[INDEX[(0,) + key[1:]]], turn, axis=1)
        by = (edge - column_of(key)) % LANES
        column = pltpu.roll(columns, by, axis=1) if by else columns
        sites[INDEX[key]] = jnp.where(lane == edge, column, moved)


def site_params(species):
    alloy = (species == 1.0).astype(jnp.float32)
    return 0.1 - 0.03 * alloy, 3.0 - 0.8 * alloy, 0.35 - 0.05 * alloy


NCOEF = 13


def tangent_kernel(
    own, xm, xp, ym, yp, cm, cp, xcm, xcp, zc, alive,
    carried, low, high, columns, coef, sites, table, geo, slope,
):
    fill_table(table)
    gather_rows(sites, CHG, own, xm, xp, ym, yp, cm, cp, xcm, xcp, zc)

    def place(j, carry):
        for d in range(DIRS):
            geo[pl.ds(d * 64 + j, 8, stride=8), :] = sites[table[j, d], CH:CHG, :]
        geo[pl.ds(DIRS * 64 + j, 8, stride=8), :] = own[j, CH:CHG, :]
        return carry

    lax.fori_loop(0, 8, place, 0)

    def quantity(d, n):
        return geo[d * 64 + n * 8 : d * 64 + n * 8 + 8, :]

    here = [quantity(DIRS, c) for c in range(3)]
    amp_here, embedding, pair_here = site_params(quantity(DIRS, 3))
    rho = jnp.zeros((8, LANES), jnp.float32)
    for d, step in enumerate(STEPS):
        amp, _, pair = site_params(quantity(d, 3))
        apart = [0.5 * lattice * step[c] + quantity(d, c) - here[c] for c in range(3)]
        distance = jnp.sqrt(apart[0] * apart[0] + apart[1] * apart[1] + apart[2] * apart[2])
        living = alive[d - NEAR] if d >= NEAR else 1.0
        inverse = 1.0 / distance
        unit = [v * inverse for v in apart]
        scaled = distance / nearest - 1.0
        density = living * jnp.exp(-density_rate * scaled)
        dens1 = -(density_rate / nearest) * density
        dens2 = (density_rate / nearest) ** 2 * density
        potential = living * pair_here * pair * jnp.exp(-repulse_rate * scaled)
        pot1 = -(repulse_rate / nearest) * potential
        pot2 = (repulse_rate / nearest) ** 2 * potential
        rho = rho + amp * density
        both = amp * dens1
        values = unit + [both * v for v in unit]
        values += [
            pot2 - pot1 * inverse, dens2 - dens1 * inverse, pot1 * inverse, dens1 * inverse,
            both, amp_here * dens1, amp,
        ]
        for n, value in enumerate(values):
            coef[d * NCOEF + n] = value
    root = jnp.sqrt(rho)
    slope[0] = -embedding / (2.0 * root)
    slope[1] = embedding / (4.0 * rho * root)

    def tangents(j, carry):
        mine = [own[j, q * 8 : q * 8 + 8, :] for q in range(12)]
        total = [jnp.zeros((8, LANES), jnp.float32) for _ in range(4)]
        for d in range(DIRS):
            at = table[j, d]
            weight = [coef[d * NCOEF + 3 + c, pl.ds(j, 1), :] for c in range(3)]
            for k in range(4):
                for c in range(3):
                    q = c * 4 + k
                    total[k] = total[k] + weight[c] * (mine[q] - sites[at, q * 8 : q * 8 + 8, :])
        scale = slope[1, pl.ds(j, 1), :]
        for k in range(4):
            carried[j, k * 8 : k * 8 + 8, :] = total[k] * scale
        carried[j, VEC : VEC + 1, :] = slope[0, pl.ds(j, 1), :]
        carried[j, VEC + 1 : WCH, :] = jnp.zeros((WCH - VEC - 1, LANES), jnp.float32)
        return carry

    lax.fori_loop(0, 8, tangents, 0)
    for s in range(4):
        low[s * WCH : (s + 1) * WCH, :] = carried[s * 2]
        high[s * WCH : (s + 1) * WCH, :] = carried[s * 2 + 1]
    columns[...] = edge_columns(WCH, carried)


def split(value):
    high = value.astype(jnp.bfloat16)
    return high, (value - high.astype(jnp.float32)).astype(jnp.bfloat16)


def mask_iota():
    row = lax.broadcasted_iota(jnp.int32, (VEC, VEC), 0)
    column = lax.broadcasted_iota(jnp.int32, (VEC, VEC), 1)
    return row, column


def packed(gram, mixed, energy):
    row, column = mask_iota()
    first = jnp.where(row <= column, gram, energy)
    even = 0.5 * (mixed + mixed.T)
    diagonal = jnp.sum(jnp.where(row == column, energy, 0.0), axis=1, keepdims=True)
    second = jnp.where(row <= column, even, jnp.where(row == column + 1, diagonal, 0.0))
    corner = jnp.broadcast_to(diagonal[0:1, :], (VEC, VEC))
    second = jnp.where((row == VEC - 1) & (column == 0), corner, second)
    half = VEC // 2
    return jnp.concatenate([first[:half], second[:half], first[half:], second[half:]], 1)


def unpacked(block):
    row, column = mask_iota()
    first = jnp.concatenate([block[:, :VEC], block[:, 2 * VEC : 3 * VEC]], 0)
    second = jnp.concatenate([block[:, VEC : 2 * VEC], block[:, 3 * VEC :]], 0)
    diagonal = jnp.sum(jnp.where(row == column + 1, second, 0.0), axis=1, keepdims=True)
    corner = jnp.broadcast_to(second[VEC - 1 :, 0:1], (VEC, 1))
    diagonal = jnp.where(row[:, 0:1] == 0, corner, diagonal)
    gram = jnp.where(row <= column, first, first.T)
    mixed = jnp.where(row <= column, second, second.T)
    energy = jnp.where(row == column, diagonal, jnp.where(row > column, first, first.T))
    return gram, mixed, energy


def image_kernel(
    own, sites, coef, w_own, w_xm, w_xp, w_ym, w_yp, w_cm, w_cp, w_xcm, w_xcp, w_zc,
    local, pieces, table, even, odd, slopes, geo, mix, sums,
):
    fill_table(table)
    gather_rows(slopes, WCH, w_own, w_xm, w_xp, w_ym, w_yp, w_cm, w_cp, w_xcm, w_xcp, w_zc)

    def place(j, carry):
        for d in range(DIRS):
            geo[d, pl.ds(j, 1), :] = slopes[table[j, d], VEC : VEC + 1, :]
        geo[DIRS, pl.ds(j, 1), :] = w_own[j, VEC : VEC + 1, :]
        geo[DIRS + 1, pl.ds(j, 1), :] = own[j, CH + 3 : CH + 4, :]
        return carry

    lax.fori_loop(0, 8, place, 0)
    slope_here = geo[DIRS]
    amp_here, _, _ = site_params(geo[DIRS + 1])
    lean = [jnp.zeros((8, LANES), jnp.float32) for _ in range(3)]
    for d in range(DIRS):
        mixing = slope_here * coef[d * NCOEF + 12] + geo[d] * amp_here
        mix[d * 2] = coef[d * NCOEF + 6] + mixing * coef[d * NCOEF + 7]
        mix[d * 2 + 1] = coef[d * NCOEF + 8] + mixing * coef[d * NCOEF + 9]
        lean = [lean[c] + coef[d * NCOEF + c] * coef[d * NCOEF + 10] for c in range(3)]
    for c in range(3):
        geo[c] = lean[c]

    sums[...] = jnp.zeros_like(sums)
    blocks = [(c, k) for c in range(3) for k in range(4)]

    def rows(j, wide_ref):
        mine = {b: own[j, (b[0] * 4 + b[1]) * 8 : (b[0] * 4 + b[1]) * 8 + 8, :] for b in blocks}
        total = {}
        for c in range(3):
            leaning = geo[c, pl.ds(j, 1), :]
            for k in range(4):
                total[(c, k)] = leaning * w_own[j, k * 8 : k * 8 + 8, :]
        for d in range(DIRS):
            at = table[j, d]
            unit = [coef[d * NCOEF + c, pl.ds(j, 1), :] for c in range(3)]
            radial = mix[d * 2, pl.ds(j, 1), :]
            across = mix[d * 2 + 1, pl.ds(j, 1), :]
            home = coef[d * NCOEF + 11, pl.ds(j, 1), :]
            for k in range(4):
                apart = [
                    mine[(c, k)] - sites[at, (c * 4 + k) * 8 : (c * 4 + k) * 8 + 8, :]
                    for c in range(3)
                ]
                along = unit[0] * apart[0] + unit[1] * apart[1] + unit[2] * apart[2]
                push = radial * along + home * slopes[at, k * 8 : k * 8 + 8, :]
                for c in range(3):
                    total[(c, k)] = total[(c, k)] + unit[c] * push + across * apart[c]
        wide = []
        for c in range(3):
            both = jnp.concatenate(
                [total[(c, k)] for k in range(4)] + [own[j, c * VEC : (c + 1) * VEC, :]], 0
            )
            wide.append(jnp.concatenate(split(both), 0))
        wide = jnp.concatenate(wide, 1)
        pieces[j] = wide
        wide_ref[...] = wide

    def products(wide_ref):
        wide = wide_ref[...]
        sums[...] += lax.dot_general(
            wide, wide, (((1,), (1,)), ((), ())), preferred_element_type=jnp.float32
        )

    def pair(i, carry):
        products(odd)
        rows(2 * i, even)
        products(even)
        rows(2 * i + 1, odd)
        return carry

    odd[...] = jnp.zeros_like(odd)
    lax.fori_loop(0, 4, pair, 0)
    products(odd)
    whole = sums[...]
    folded = whole[: 2 * VEC] + whole[2 * VEC :]
    folded = folded[:, : 2 * VEC] + folded[:, 2 * VEC :]
    block = packed(folded[VEC:, VEC:], folded[VEC:, :VEC], folded[:VEC, :VEC])
    for i in range(local.shape[0]):
        local[i] = block


def add_kernel(parts, out):
    total = parts[0]
    for i in range(1, parts.shape[0]):
        total = total + parts[i]
    for i in range(out.shape[0]):
        out[i] = total


def factor(gram):
    row, column = mask_iota()
    work = jnp.concatenate(
        [gram, (row == column).astype(jnp.float32), jnp.zeros((VEC, 2 * VEC), jnp.float32)], 1
    )
    below = lax.broadcasted_iota(jnp.int32, (VEC, LANES), 0)
    pivots = jnp.zeros((VEC, LANES), jnp.float32)
    for k in range(0, VEC, 4):
        sides = [jnp.broadcast_to(work[:, k + p : k + p + 1], (VEC, LANES)) for p in range(4)]
        tops = [work[k + p : k + p + 1, :] for p in range(4)]
        for p in range(4):
            at = k + p
            pivots = jnp.where(below == at, sides[p], pivots)
            ratio = jnp.where(below > at, sides[p] * (1.0 / sides[p][at : at + 1, :]), 0.0)
            for q in range(p + 1, 4):
                tops[q] = tops[q] - ratio[k + q : k + q + 1, :] * tops[p]
                sides[q] = sides[q] - ratio * sides[p][k + q : k + q + 1, :]
            work = work - ratio * tops[p]
    return (work * (1.0 / jnp.sqrt(pivots)))[:, VEC : 2 * VEC]


def exact(a, b, dims):
    return lax.dot_general(
        a, b, (dims, ((), ())), precision=lax.Precision.HIGHEST, preferred_element_type=jnp.float32
    )


def residual_kernel(
    count_all, parts, pieces, residual_hbm, projected, rms, lost, here, residual, sems
):
    total = parts[0]
    for i in range(1, parts.shape[0]):
        total = total + parts[i]
    gram, mixed, energy = unpacked(total / count_all)
    inverse = factor(gram)
    turned = exact(inverse, jnp.concatenate([mixed, energy], 1), ((1,), (0,)))
    raw = exact(turned[:, :VEC], inverse, ((1,), (1,)))
    sym = 0.5 * (raw + raw.T)
    projected[...] = sym
    right = exact(sym, inverse, ((1,), (0,)))
    high, low = split(jnp.concatenate([inverse, -right], 1))
    left = jnp.concatenate([high, high, low], 1)
    total = jnp.zeros((VEC, LANES), jnp.float32)
    copies = []
    for c in range(3):
        for j in range(8):
            block = pieces[j, :, c * LANES : (c + 1) * LANES]
            value = jnp.dot(
                left,
                jnp.concatenate([block, block[: 2 * VEC]], 0),
                preferred_element_type=jnp.float32,
            )
            residual[pl.ds(c * VEC * 8 + j, VEC, stride=8), :] = value
            total = total + value * value
        part = pl.ds(c * VEC * 8, VEC * 8)
        copies.append(pltpu.make_async_copy(residual.at[part], residual_hbm.at[part], sems.at[c]))
        copies[-1].start()
    norms = jnp.sum(turned[:, VEC:] * inverse, axis=1, keepdims=True)
    left_over = norms - jnp.sum(sym * sym, axis=1, keepdims=True)
    wide = jnp.concatenate(
        [
            jnp.broadcast_to(jnp.sqrt(left_over + epsilon), (VEC, LANES)),
            jnp.broadcast_to(jnp.sum(total, axis=1, keepdims=True), (VEC, LANES)),
            jnp.zeros((LANES - 2 * VEC, LANES), jnp.float32),
        ],
        0,
    ).T
    rms[...] = wide[0:1, :VEC]
    here[...] = wide[0:1, VEC : 2 * VEC]
    kept = jnp.where(left_over > 0.02 * norms, 0, 1)
    lost[0, 0] = jnp.max(kept)
    for copy in copies:
        copy.wait()


def shift(value, axis, by):
    axis = ("ga", "gb") if axis == "gy" else axis
    peers = peers_of(axis) if isinstance(axis, tuple) else lax.axis_size(axis)
    return lax.ppermute(value, axis, [(i, (i + by) % peers) for i in range(peers)])


def exchanged(parts, axes):
    return lax.all_to_all(parts, axes, 0, 0, tiled=False)


def halo(channels, own, low, high, columns):
    ym, yp = shift(high, "gy", 1), shift(low, "gy", -1)
    zm, zp = shift(columns, "gz", 1), shift(columns, "gz", -1)
    xm, xp = shift(own, "gx", 1), shift(own, "gx", -1)
    row = lax.broadcasted_iota(jnp.int32, columns.shape, 0)
    zc = jnp.where(row < 8, zp, zm)

    def corners(side, y):
        rows = [(xm, CORNER[(-1, side)] * 2 + y), (xp, CORNER[(1, side)] * 2 + y)]
        return jnp.concatenate([face[j] for face, j in rows] + [zc], 0)

    cm, cp = shift(corners(Y_LOW, 1), "gy", 1), shift(corners(Y_HIGH, 0), "gy", -1)
    xcm, xcp = shift(zc, "gx", 1), shift(zc, "gx", -1)
    return xm, xp, ym, yp, cm, cp, xcm, xcp, zc


FIRST, SECOND = ("gx",), ("ga", "gb", "gz")


def peers_of(axes):
    return math.prod(lax.axis_size(axis) for axis in axes)


def body(trial_block, site_shift, species, neighbours, counts):
    first, second = peers_of(FIRST), peers_of(SECOND)
    count_all = 3.0 * 1024 * first * second
    vmem = lambda shape, dtype=jnp.float32: pltpu.VMEM(shape, dtype)
    lists = neighbours.reshape(-1, 8, LANES)
    edge = (16, LANES)
    table = pltpu.SMEM((8, DIRS), jnp.int32)
    own, low, high, columns, alive = call(
        own_rows_kernel,
        ((8, CHG, LANES), (4 * CHG, LANES), (4 * CHG, LANES), edge, (DIRS - NEAR, 8, LANES)),
        (
            trial_block.reshape(CH * 8, LANES),
            site_shift.reshape(3, 8, LANES),
            species.reshape(8, LANES),
            lists,
            counts.reshape(8, LANES),
        ),
        scratch=[
            vmem((CH * 8, LANES)), vmem((3, 8, LANES)), vmem((8, LANES), jnp.int32),
            vmem(lists.shape, jnp.int32), vmem((8, LANES), jnp.int32),
            pltpu.SemaphoreType.DMA((7,)),
        ],
        hbm=(0, 1, 2, 3, 4),
        name="own_rows",
        limit=60 * 1024 * 1024,
    )
    around = halo(CHG, own, low, high, columns)
    own, alive = call(
        bring_kernel, (own.shape, alive.shape), (own, alive, around[-1]), name="bring"
    )
    carried, low_w, high_w, columns_w, coef, sites = call(
        tangent_kernel,
        (
            (8, WCH, LANES), (4 * WCH, LANES), (4 * WCH, LANES), edge, (DIRS * NCOEF, 8, LANES),
            (len(ROWS), CHG, LANES),
        ),
        (own,) + around + (alive,),
        scratch=[table, vmem(((DIRS + 1) * 64, LANES)), vmem((2, 8, LANES))],
        name="tangents",
    )
    around_w = halo(WCH, carried, low_w, high_w, columns_w)
    local, pieces = call(
        image_kernel,
        ((first, VEC // 2, LANES), (8, 4 * VEC, 3 * LANES, jnp.bfloat16)),
        (own, sites, coef, carried) + around_w,
        scratch=[
            table, vmem((4 * VEC, 3 * LANES), jnp.bfloat16),
            vmem((4 * VEC, 3 * LANES), jnp.bfloat16), vmem((len(ROWS), WCH, LANES)),
            vmem((DIRS + 2, 8, LANES)), vmem((DIRS * 2, 8, LANES)), vmem((4 * VEC, 4 * VEC)),
        ],
        name="images",
    )
    (group,) = call(
        add_kernel, ((second, VEC // 2, LANES),), (exchanged(local, FIRST),), name="group_sum"
    )

    def kernel(*refs):
        residual_kernel(count_all, *refs)

    residual, projected, rms, lost, here = call(
        kernel,
        ((CH * 8, LANES), (VEC, VEC), (1, VEC), (1, 1, jnp.int32), (1, VEC)),
        (exchanged(group, SECOND), pieces),
        scratch=[vmem((CH * 8, LANES)), pltpu.SemaphoreType.DMA((3,))],
        hbm_outs=(0,),
        smem_outs=(3,),
        name="residuals",
    )
    rms = lax.cond(
        lost[0, 0] != 0,
        lambda: jnp.sqrt(lax.psum(here, FIRST + SECOND) / count_all + epsilon),
        lambda: rms,
    )
    return residual.reshape(trial_block.shape), projected, rms.reshape(VEC)


def solution(mesh):
    grid = mesh.devices
    halves = jax.sharding.Mesh(
        grid.reshape(grid.shape[0], 2, grid.shape[1] // 2, grid.shape[2]), ("gx", "ga", "gb", "gz")
    )
    cells = ("gx", ("ga", "gb"), "gz")
    placed = (
        P(None, None, *cells),
        P(None, None, *cells),
        P(None, *cells),
        P(None, None, *cells),
        P(None, *cells),
    )
    return jax.shard_map(
        body,
        mesh=halves,
        in_specs=placed,
        out_specs=(P(None, None, *cells), P(), P()),
        check_vma=False,
    )
```

```python
import math

import jax
import jax.numpy as jnp
from jax import lax
from jax.experimental import pallas as pl
from jax.experimental.pallas import tpu as pltpu
from jax.sharding import PartitionSpec as P

lattice = 3.52
nearest = 3.52 / math.sqrt(2.0)
density_rate = 5.0
repulse_rate = 9.0
epsilon = 1e-06
vmem_bytes = 40 * 1024 * 1024

VEC = 32
CH = 3 * VEC
CHG = CH + 8
WCH = VEC + 8
LANES = 128
BITS = ((0, 0, 0), (1, 1, 0), (1, 0, 1), (0, 1, 1))


def directions():
    steps = []
    for p in range(3):
        for q in range(p + 1, 3):
            for a in (1, -1):
                for b in (1, -1):
                    step = [0, 0, 0]
                    step[p], step[q] = a, b
                    steps.append(tuple(step))
    for p in range(3):
        for a in (2, -2):
            step = [0, 0, 0]
            step[p] = a
            steps.append(tuple(step))
    return steps


STEPS = directions()
DIRS = len(STEPS)
NEAR = 12


def partner(sub, step):
    summed = [BITS[sub][c] + step[c] for c in range(3)]
    return BITS.index(tuple(v % 2 for v in summed)), tuple(v // 2 for v in summed)


def site_table():
    plain, shifted, table = [], [], {}
    for sub in range(4):
        for y in range(2):
            plain.append((0, 0, y, sub))
    for sub in range(4):
        for y in range(2):
            for d, step in enumerate(STEPS):
                other, off = partner(sub, step)
                key = (off[2], off[0], y + off[1], other)
                table[(sub, y, d)] = key
                base = (0,) + key[1:]
                if base not in plain:
                    plain.append(base)
                if key[0] != 0 and key not in shifted:
                    shifted.append(key)
    return plain, shifted, table


PLAIN, SHIFTED, TABLE = site_table()
ROWS = PLAIN + SHIFTED
INDEX = {key: i for i, key in enumerate(ROWS)}
Y_LOW, Y_HIGH = -1, 2


def bring_kernel(own_in, alive_in, after, own, alive):
    own[...] = own_in[...]
    alive[...] = alive_in[...]


def fill_table(table):
    for j in range(8):
        for d in range(DIRS):
            table[j, d] = INDEX[TABLE[(j // 2, j % 2, d)]]


def even(axis):
    return lax.rem(lax.axis_index("gb" if axis == "gy" else axis), 2) == 0


def source(key, channels, own, xa, xb, ya, yb, ca, cb):
    _, x, y, sub = key
    if x == 0 and 0 <= y < 2:
        return own[sub * 2 + y]
    if 0 <= y < 2:
        j = sub * 2 + y
        return jnp.where(even("gx") == (x > 0), xa[j], xb[j])
    if x == 0:
        first, second, place = ya, yb, sub * channels
    else:
        first, second, place = ca, cb, 0 if x < 0 else channels
    part = slice(place, place + channels)
    return jnp.where(even("gy") == (y > 0), first[part, :], second[part, :])


def column_of(key):
    sz, x, y, sub = key
    group = {(-1, 0): 1, (1, 0): 2, (0, -1): 3, (0, 1): 4, (0, 0): 0}[
        (x, 0 if 0 <= y < 2 else (-1 if y < 0 else 1))
    ]
    return group * 16 + (0 if sz == 1 else 8) + sub * 2 + y % 2


CORNER = {}
for _key in PLAIN:
    if _key[1] != 0 and not 0 <= _key[2] < 2:
        CORNER[(_key[1], _key[2])] = _key[3]


def call(kernel, outs, args, scratch=(), hbm=(), hbm_outs=(), smem_outs=(), name=None, limit=vmem_bytes):
    outs = [s + (jnp.float32,) if isinstance(s[-1], int) else s for s in outs]
    spaces = [
        pltpu.HBM if i in hbm_outs else pltpu.SMEM if i in smem_outs else pltpu.VMEM
        for i in range(len(outs))
    ]
    return pl.pallas_call(
        kernel,
        out_shape=tuple(jax.ShapeDtypeStruct(s[:-1], s[-1]) for s in outs),
        in_specs=[
            pl.BlockSpec(memory_space=pltpu.HBM if i in hbm else pltpu.VMEM)
            for i in range(len(args))
        ],
        out_specs=tuple(pl.BlockSpec(memory_space=space) for space in spaces),
        scratch_shapes=list(scratch),
        compiler_params=pltpu.CompilerParams(vmem_limit_bytes=limit),
        name=name,
    )(*args)


def own_rows_kernel(
    trial_hbm, shift_hbm, species_hbm, lists_hbm, counts_hbm,
    own, low, high, columns, alive, trial, shift, species, lists, counts, sems,
):
    copies = [
        pltpu.make_async_copy(shift_hbm, shift, sems.at[0]),
        pltpu.make_async_copy(species_hbm, species, sems.at[1]),
    ]
    for c in range(3):
        part = pl.ds(c * VEC * 8, VEC * 8)
        copies.append(pltpu.make_async_copy(trial_hbm.at[part], trial.at[part], sems.at[2 + c]))
    copies.append(pltpu.make_async_copy(lists_hbm, lists, sems.at[5]))
    copies.append(pltpu.make_async_copy(counts_hbm, counts, sems.at[6]))
    for copy in copies:
        copy.start()

    def small(j, carry):
        for c in range(3):
            own[j, CH + c : CH + c + 1, :] = shift[c, pl.ds(j, 1), :]
        own[j, CH + 3 : CH + 4, :] = species[pl.ds(j, 1), :].astype(jnp.float32)
        own[j, CH + 4 : CHG, :] = jnp.zeros((4, LANES), jnp.float32)
        return carry

    copies[0].wait()
    copies[1].wait()
    lax.fori_loop(0, 8, small, 0)
    for c in range(3):

        def large(j, carry):
            own[j, c * VEC : (c + 1) * VEC, :] = trial[pl.ds(c * VEC * 8 + j, VEC, stride=8), :]
            return carry

        copies[2 + c].wait()
        lax.fori_loop(0, 8, large, 0)
    for sub in range(4):
        part = slice(sub * CHG, (sub + 1) * CHG)
        low[part, :] = jnp.where(even("gy"), own[sub * 2], own[sub * 2 + 1])
        high[part, :] = jnp.where(even("gy"), own[sub * 2 + 1], own[sub * 2])
    columns[...] = edge_columns(CHG, own)
    copies[5].wait()
    copies[6].wait()
    row = lax.broadcasted_iota(jnp.int32, (8, LANES), 0)
    lane = lax.broadcasted_iota(jnp.int32, (8, LANES), 1)
    sub, y = row // 2, row % 2
    live = counts[...]
    listed = [jnp.where(m < live, lists[m], -1) for m in range(lists.shape[0])]
    for i, step in enumerate(STEPS[NEAR:]):
        off = [v // 2 for v in step]
        expected = ((sub * 3 + 1 + off[0]) * 4 + y + 1 + off[1]) * 130 + lane + 1 + off[2]
        found = listed[0] == expected
        for m in range(1, len(listed)):
            found = found | (listed[m] == expected)
        alive[i] = found.astype(jnp.float32)


def edge_columns(channels, own):
    lane = lax.broadcasted_iota(jnp.int32, (channels, LANES), 1)
    total = jnp.zeros((channels, LANES), jnp.float32)
    for j in range(8):
        row = own[j]
        total = jnp.where(lane == j, pltpu.roll(row, j, axis=1) if j else row, total)
        total = jnp.where(lane == 8 + j, pltpu.roll(row, 9 + j, axis=1), total)
    full = jnp.concatenate([total, jnp.zeros((LANES - channels, LANES), jnp.float32)], 0)
    return full.T[:16]


def gather_rows(sites, channels, own, xa, xb, ya, yb, ca, cb, xca, xcb, zc):
    lane = lax.broadcasted_iota(jnp.int32, (channels, LANES), 1)
    for i, key in enumerate(PLAIN):
        sites[i] = source(key, channels, own, xa, xb, ya, yb, ca, cb)
    groups = [zc[...]]
    for up in (False, True):
        groups.append(jnp.where(even("gx") == up, xca[...], xcb[...]))
    for up in (False, True):
        side = slice(2 * channels, 2 * channels + 16)
        groups.append(jnp.where(even("gy") == up, ca[side, :], cb[side, :]))
    groups.append(jnp.zeros((LANES - 80, LANES), jnp.float32))
    columns = jnp.concatenate(groups, 0).T[:channels]
    for key in SHIFTED:
        turn, edge = (LANES - 1, LANES - 1) if key[0] == 1 else (1, 0)
        moved = pltpu.roll(sites[INDEX[(0,) + key[1:]]], turn, axis=1)
        by = (edge - column_of(key)) % LANES
        column = pltpu.roll(columns, by, axis=1) if by else columns
        sites[INDEX[key]] = jnp.where(lane == edge, column, moved)


def site_params(species):
    alloy = (species == 1.0).astype(jnp.float32)
    return 0.1 - 0.03 * alloy, 3.0 - 0.8 * alloy, 0.35 - 0.05 * alloy


NCOEF = 13


def tangent_kernel(
    own, xa, xb, ya, yb, ca, cb, xca, xcb, zc, alive,
    carried, low, high, columns, coef, sites, table, geo, slope,
):
    fill_table(table)
    gather_rows(sites, CHG, own, xa, xb, ya, yb, ca, cb, xca, xcb, zc)

    def place(j, carry):
        for d in range(DIRS):
            geo[pl.ds(d * 64 + j, 8, stride=8), :] = sites[table[j, d], CH:CHG, :]
        geo[pl.ds(DIRS * 64 + j, 8, stride=8), :] = own[j, CH:CHG, :]
        return carry

    lax.fori_loop(0, 8, place, 0)

    def quantity(d, n):
        return geo[d * 64 + n * 8 : d * 64 + n * 8 + 8, :]

    here = [quantity(DIRS, c) for c in range(3)]
    amp_here, embedding, pair_here = site_params(quantity(DIRS, 3))
    rho = jnp.zeros((8, LANES), jnp.float32)
    for d, step in enumerate(STEPS):
        amp, _, pair = site_params(quantity(d, 3))
        apart = [0.5 * lattice * step[c] + quantity(d, c) - here[c] for c in range(3)]
        distance = jnp.sqrt(apart[0] * apart[0] + apart[1] * apart[1] + apart[2] * apart[2])
        living = alive[d - NEAR] if d >= NEAR else 1.0
        inverse = 1.0 / distance
        unit = [v * inverse for v in apart]
        scaled = distance / nearest - 1.0
        density = living * jnp.exp(-density_rate * scaled)
        dens1 = -(density_rate / nearest) * density
        dens2 = (density_rate / nearest) ** 2 * density
        potential = living * pair_here * pair * jnp.exp(-repulse_rate * scaled)
        pot1 = -(repulse_rate / nearest) * potential
        pot2 = (repulse_rate / nearest) ** 2 * potential
        rho = rho + amp * density
        both = amp * dens1
        values = unit + [both * v for v in unit]
        values += [
            pot2 - pot1 * inverse, dens2 - dens1 * inverse, pot1 * inverse, dens1 * inverse,
            both, amp_here * dens1, amp,
        ]
        for n, value in enumerate(values):
            coef[d * NCOEF + n] = value
    root = jnp.sqrt(rho)
    slope[0] = -embedding / (2.0 * root)
    slope[1] = embedding / (4.0 * rho * root)

    def tangents(j, carry):
        mine = [own[j, q * 8 : q * 8 + 8, :] for q in range(12)]
        total = [jnp.zeros((8, LANES), jnp.float32) for _ in range(4)]
        for d in range(DIRS):
            at = table[j, d]
            weight = [coef[d * NCOEF + 3 + c, pl.ds(j, 1), :] for c in range(3)]
            for k in range(4):
                for c in range(3):
                    q = c * 4 + k
                    total[k] = total[k] + weight[c] * (mine[q] - sites[at, q * 8 : q * 8 + 8, :])
        scale = slope[1, pl.ds(j, 1), :]
        for k in range(4):
            carried[j, k * 8 : k * 8 + 8, :] = total[k] * scale
        carried[j, VEC : VEC + 1, :] = slope[0, pl.ds(j, 1), :]
        carried[j, VEC + 1 : WCH, :] = jnp.zeros((WCH - VEC - 1, LANES), jnp.float32)
        return carry

    lax.fori_loop(0, 8, tangents, 0)
    for s in range(4):
        part = slice(s * WCH, (s + 1) * WCH)
        low[part, :] = jnp.where(even("gy"), carried[s * 2], carried[s * 2 + 1])
        high[part, :] = jnp.where(even("gy"), carried[s * 2 + 1], carried[s * 2])
    columns[...] = edge_columns(WCH, carried)


def split(value):
    high = value.astype(jnp.bfloat16)
    return high, (value - high.astype(jnp.float32)).astype(jnp.bfloat16)


def mask_iota():
    row = lax.broadcasted_iota(jnp.int32, (VEC, VEC), 0)
    column = lax.broadcasted_iota(jnp.int32, (VEC, VEC), 1)
    return row, column


def packed(gram, mixed, energy):
    row, column = mask_iota()
    first = jnp.where(row <= column, gram, energy)
    even = 0.5 * (mixed + mixed.T)
    diagonal = jnp.sum(jnp.where(row == column, energy, 0.0), axis=1, keepdims=True)
    second = jnp.where(row <= column, even, jnp.where(row == column + 1, diagonal, 0.0))
    corner = jnp.broadcast_to(diagonal[0:1, :], (VEC, VEC))
    second = jnp.where((row == VEC - 1) & (column == 0), corner, second)
    half = VEC // 2
    return jnp.concatenate([first[:half], second[:half], first[half:], second[half:]], 1)


def unpacked(block):
    row, column = mask_iota()
    first = jnp.concatenate([block[:, :VEC], block[:, 2 * VEC : 3 * VEC]], 0)
    second = jnp.concatenate([block[:, VEC : 2 * VEC], block[:, 3 * VEC :]], 0)
    diagonal = jnp.sum(jnp.where(row == column + 1, second, 0.0), axis=1, keepdims=True)
    corner = jnp.broadcast_to(second[VEC - 1 :, 0:1], (VEC, 1))
    diagonal = jnp.where(row[:, 0:1] == 0, corner, diagonal)
    gram = jnp.where(row <= column, first, first.T)
    mixed = jnp.where(row <= column, second, second.T)
    energy = jnp.where(row == column, diagonal, jnp.where(row > column, first, first.T))
    return gram, mixed, energy


def image_kernel(
    own, sites, coef, w_own, w_xa, w_xb, w_ya, w_yb, w_ca, w_cb, w_xca, w_xcb, w_zc,
    local, pieces, table, even, odd, slopes, geo, mix, sums,
):
    fill_table(table)
    gather_rows(slopes, WCH, w_own, w_xa, w_xb, w_ya, w_yb, w_ca, w_cb, w_xca, w_xcb, w_zc)

    def place(j, carry):
        for d in range(DIRS):
            geo[d, pl.ds(j, 1), :] = slopes[table[j, d], VEC : VEC + 1, :]
        geo[DIRS, pl.ds(j, 1), :] = w_own[j, VEC : VEC + 1, :]
        geo[DIRS + 1, pl.ds(j, 1), :] = own[j, CH + 3 : CH + 4, :]
        return carry

    lax.fori_loop(0, 8, place, 0)
    slope_here = geo[DIRS]
    amp_here, _, _ = site_params(geo[DIRS + 1])
    lean = [jnp.zeros((8, LANES), jnp.float32) for _ in range(3)]
    for d in range(DIRS):
        mixing = slope_here * coef[d * NCOEF + 12] + geo[d] * amp_here
        mix[d * 2] = coef[d * NCOEF + 6] + mixing * coef[d * NCOEF + 7]
        mix[d * 2 + 1] = coef[d * NCOEF + 8] + mixing * coef[d * NCOEF + 9]
        lean = [lean[c] + coef[d * NCOEF + c] * coef[d * NCOEF + 10] for c in range(3)]
    for c in range(3):
        geo[c] = lean[c]

    sums[...] = jnp.zeros_like(sums)
    blocks = [(c, k) for c in range(3) for k in range(4)]

    def rows(j, wide_ref):
        mine = {b: own[j, (b[0] * 4 + b[1]) * 8 : (b[0] * 4 + b[1]) * 8 + 8, :] for b in blocks}
        total = {}
        for c in range(3):
            leaning = geo[c, pl.ds(j, 1), :]
            for k in range(4):
                total[(c, k)] = leaning * w_own[j, k * 8 : k * 8 + 8, :]
        for d in range(DIRS):
            at = table[j, d]
            unit = [coef[d * NCOEF + c, pl.ds(j, 1), :] for c in range(3)]
            radial = mix[d * 2, pl.ds(j, 1), :]
            across = mix[d * 2 + 1, pl.ds(j, 1), :]
            home = coef[d * NCOEF + 11, pl.ds(j, 1), :]
            for k in range(4):
                apart = [
                    mine[(c, k)] - sites[at, (c * 4 + k) * 8 : (c * 4 + k) * 8 + 8, :]
                    for c in range(3)
                ]
                along = unit[0] * apart[0] + unit[1] * apart[1] + unit[2] * apart[2]
                push = radial * along + home * slopes[at, k * 8 : k * 8 + 8, :]
                for c in range(3):
                    total[(c, k)] = total[(c, k)] + unit[c] * push + across * apart[c]
        wide = []
        for c in range(3):
            both = jnp.concatenate(
                [total[(c, k)] for k in range(4)] + [own[j, c * VEC : (c + 1) * VEC, :]], 0
            )
            wide.append(jnp.concatenate(split(both), 0))
        wide = jnp.concatenate(wide, 1)
        pieces[j] = wide
        wide_ref[...] = wide

    def products(wide_ref):
        wide = wide_ref[...]
        sums[...] += lax.dot_general(
            wide, wide, (((1,), (1,)), ((), ())), preferred_element_type=jnp.float32
        )

    def pair(i, carry):
        products(odd)
        rows(2 * i, even)
        products(even)
        rows(2 * i + 1, odd)
        return carry

    odd[...] = jnp.zeros_like(odd)
    lax.fori_loop(0, 4, pair, 0)
    products(odd)
    whole = sums[...]
    folded = whole[: 2 * VEC] + whole[2 * VEC :]
    folded = folded[:, : 2 * VEC] + folded[:, 2 * VEC :]
    block = packed(folded[VEC:, VEC:], folded[VEC:, :VEC], folded[:VEC, :VEC])
    for i in range(local.shape[0]):
        local[i] = block


def add_kernel(parts, out):
    total = parts[0]
    for i in range(1, parts.shape[0]):
        total = total + parts[i]
    for i in range(out.shape[0]):
        out[i] = total


def factor(gram):
    row, column = mask_iota()
    work = jnp.concatenate(
        [gram, (row == column).astype(jnp.float32), jnp.zeros((VEC, 2 * VEC), jnp.float32)], 1
    )
    below = lax.broadcasted_iota(jnp.int32, (VEC, LANES), 0)
    pivots = jnp.zeros((VEC, LANES), jnp.float32)
    for k in range(0, VEC, 4):
        sides = [jnp.broadcast_to(work[:, k + p : k + p + 1], (VEC, LANES)) for p in range(4)]
        tops = [work[k + p : k + p + 1, :] for p in range(4)]
        for p in range(4):
            at = k + p
            pivots = jnp.where(below == at, sides[p], pivots)
            ratio = jnp.where(below > at, sides[p] * (1.0 / sides[p][at : at + 1, :]), 0.0)
            for q in range(p + 1, 4):
                tops[q] = tops[q] - ratio[k + q : k + q + 1, :] * tops[p]
                sides[q] = sides[q] - ratio * sides[p][k + q : k + q + 1, :]
            work = work - ratio * tops[p]
    return (work * (1.0 / jnp.sqrt(pivots)))[:, VEC : 2 * VEC]


def exact(a, b, dims):
    return lax.dot_general(
        a, b, (dims, ((), ())), precision=lax.Precision.HIGHEST, preferred_element_type=jnp.float32
    )


def residual_kernel(
    count_all, parts, pieces, residual_hbm, projected, rms, lost, here, residual, sems
):
    total = parts[0]
    for i in range(1, parts.shape[0]):
        total = total + parts[i]
    gram, mixed, energy = unpacked(total / count_all)
    inverse = factor(gram)
    turned = exact(inverse, jnp.concatenate([mixed, energy], 1), ((1,), (0,)))
    raw = exact(turned[:, :VEC], inverse, ((1,), (1,)))
    sym = 0.5 * (raw + raw.T)
    projected[...] = sym
    right = exact(sym, inverse, ((1,), (0,)))
    high, low = split(jnp.concatenate([inverse, -right], 1))
    left = jnp.concatenate([high, high, low], 1)
    total = jnp.zeros((VEC, LANES), jnp.float32)
    copies = []
    for c in range(3):
        for j in range(8):
            block = pieces[j, :, c * LANES : (c + 1) * LANES]
            value = jnp.dot(
                left,
                jnp.concatenate([block, block[: 2 * VEC]], 0),
                preferred_element_type=jnp.float32,
            )
            residual[pl.ds(c * VEC * 8 + j, VEC, stride=8), :] = value
            total = total + value * value
        part = pl.ds(c * VEC * 8, VEC * 8)
        copies.append(pltpu.make_async_copy(residual.at[part], residual_hbm.at[part], sems.at[c]))
        copies[-1].start()
    norms = jnp.sum(turned[:, VEC:] * inverse, axis=1, keepdims=True)
    left_over = norms - jnp.sum(sym * sym, axis=1, keepdims=True)
    wide = jnp.concatenate(
        [
            jnp.broadcast_to(jnp.sqrt(left_over + epsilon), (VEC, LANES)),
            jnp.broadcast_to(jnp.sum(total, axis=1, keepdims=True), (VEC, LANES)),
            jnp.zeros((LANES - 2 * VEC, LANES), jnp.float32),
        ],
        0,
    ).T
    rms[...] = wide[0:1, :VEC]
    here[...] = wide[0:1, VEC : 2 * VEC]
    kept = jnp.where(left_over > 0.02 * norms, 0, 1)
    lost[0, 0] = jnp.max(kept)
    for copy in copies:
        copy.wait()


def met(first, second, axis):
    axes = ("ga", "gb") if axis == "gy" else (axis,)
    peers = peers_of(axes)
    pairs = [(i, i ^ 1) for i in range(peers)]
    others = [(i, (i + 1) % peers if i % 2 else (i - 1) % peers) for i in range(peers)]
    return lax.ppermute(first, axes, pairs), lax.ppermute(second, axes, others)


def exchanged(parts, axes):
    return lax.all_to_all(parts, axes, 0, 0, tiled=False)


def halo(channels, own, low, high, columns):
    ya, yb = met(high, low, "gy")
    za, zb = met(columns, columns, "gz")
    xa, xb = met(own, own, "gx")
    row = lax.broadcasted_iota(jnp.int32, columns.shape, 0)
    zc = jnp.where((row < 8) == even("gz"), za, zb)

    def corners(side, y):
        below, above = CORNER[(-1, side)] * 2 + y, CORNER[(1, side)] * 2 + y
        return [
            jnp.where(even("gx"), xb[below], xa[below]),
            jnp.where(even("gx"), xa[above], xb[above]),
        ]

    up, down = corners(Y_LOW, 1), corners(Y_HIGH, 0)
    first = [jnp.where(even("gy"), u, d) for u, d in zip(up, down)]
    second = [jnp.where(even("gy"), d, u) for u, d in zip(up, down)]
    ca, cb = met(jnp.concatenate(first + [zc], 0), jnp.concatenate(second + [zc], 0), "gy")
    xca, xcb = met(zc, zc, "gx")
    return xa, xb, ya, yb, ca, cb, xca, xcb, zc


FIRST, SECOND = ("gx",), ("ga", "gb", "gz")


def peers_of(axes):
    return math.prod(lax.axis_size(axis) for axis in axes)


def body(trial_block, site_shift, species, neighbours, counts):
    first, second = peers_of(FIRST), peers_of(SECOND)
    count_all = 3.0 * 1024 * first * second
    vmem = lambda shape, dtype=jnp.float32: pltpu.VMEM(shape, dtype)
    lists = neighbours.reshape(-1, 8, LANES)
    edge = (16, LANES)
    table = pltpu.SMEM((8, DIRS), jnp.int32)
    own, low, high, columns, alive = call(
        own_rows_kernel,
        ((8, CHG, LANES), (4 * CHG, LANES), (4 * CHG, LANES), edge, (DIRS - NEAR, 8, LANES)),
        (
            trial_block.reshape(CH * 8, LANES),
            site_shift.reshape(3, 8, LANES),
            species.reshape(8, LANES),
            lists,
            counts.reshape(8, LANES),
        ),
        scratch=[
            vmem((CH * 8, LANES)), vmem((3, 8, LANES)), vmem((8, LANES), jnp.int32),
            vmem(lists.shape, jnp.int32), vmem((8, LANES), jnp.int32),
            pltpu.SemaphoreType.DMA((7,)),
        ],
        hbm=(0, 1, 2, 3, 4),
        name="own_rows",
        limit=60 * 1024 * 1024,
    )
    around = halo(CHG, own, low, high, columns)
    own, alive = call(
        bring_kernel, (own.shape, alive.shape), (own, alive, around[-1]), name="bring"
    )
    carried, low_w, high_w, columns_w, coef, sites = call(
        tangent_kernel,
        (
            (8, WCH, LANES), (4 * WCH, LANES), (4 * WCH, LANES), edge, (DIRS * NCOEF, 8, LANES),
            (len(ROWS), CHG, LANES),
        ),
        (own,) + around + (alive,),
        scratch=[table, vmem(((DIRS + 1) * 64, LANES)), vmem((2, 8, LANES))],
        name="tangents",
    )
    around_w = halo(WCH, carried, low_w, high_w, columns_w)
    local, pieces = call(
        image_kernel,
        ((first, VEC // 2, LANES), (8, 4 * VEC, 3 * LANES, jnp.bfloat16)),
        (own, sites, coef, carried) + around_w,
        scratch=[
            table, vmem((4 * VEC, 3 * LANES), jnp.bfloat16),
            vmem((4 * VEC, 3 * LANES), jnp.bfloat16), vmem((len(ROWS), WCH, LANES)),
            vmem((DIRS + 2, 8, LANES)), vmem((DIRS * 2, 8, LANES)), vmem((4 * VEC, 4 * VEC)),
        ],
        name="images",
    )
    (group,) = call(
        add_kernel, ((second, VEC // 2, LANES),), (exchanged(local, FIRST),), name="group_sum"
    )

    def kernel(*refs):
        residual_kernel(count_all, *refs)

    residual, projected, rms, lost, here = call(
        kernel,
        ((CH * 8, LANES), (VEC, VEC), (1, VEC), (1, 1, jnp.int32), (1, VEC)),
        (exchanged(group, SECOND), pieces),
        scratch=[vmem((CH * 8, LANES)), pltpu.SemaphoreType.DMA((3,))],
        hbm_outs=(0,),
        smem_outs=(3,),
        name="residuals",
    )
    rms = lax.cond(
        lost[0, 0] != 0,
        lambda: jnp.sqrt(lax.psum(here, FIRST + SECOND) / count_all + epsilon),
        lambda: rms,
    )
    return residual.reshape(trial_block.shape), projected, rms.reshape(VEC)


def solution(mesh):
    grid = mesh.devices
    halves = jax.sharding.Mesh(
        grid.reshape(grid.shape[0], 2, grid.shape[1] // 2, grid.shape[2]), ("gx", "ga", "gb", "gz")
    )
    cells = ("gx", ("ga", "gb"), "gz")
    placed = (
        P(None, None, *cells),
        P(None, None, *cells),
        P(None, *cells),
        P(None, None, *cells),
        P(None, *cells),
    )
    return jax.shard_map(
        body,
        mesh=halves,
        in_specs=placed,
        out_specs=(P(None, None, *cells), P(), P()),
        check_vma=False,
    )
```

```python
import math

import jax
import jax.numpy as jnp
from jax import lax
from jax.experimental import pallas as pl
from jax.experimental.pallas import tpu as pltpu
from jax.sharding import PartitionSpec as P

lattice = 3.52
nearest = 3.52 / math.sqrt(2.0)
density_rate = 5.0
repulse_rate = 9.0
epsilon = 1e-06
vmem_bytes = 40 * 1024 * 1024

VEC = 32
CH = 3 * VEC
CHG = CH + 8
WCH = VEC + 8
LANES = 128
BITS = ((0, 0, 0), (1, 1, 0), (1, 0, 1), (0, 1, 1))


def directions():
    steps = []
    for p in range(3):
        for q in range(p + 1, 3):
            for a in (1, -1):
                for b in (1, -1):
                    step = [0, 0, 0]
                    step[p], step[q] = a, b
                    steps.append(tuple(step))
    for p in range(3):
        for a in (2, -2):
            step = [0, 0, 0]
            step[p] = a
            steps.append(tuple(step))
    return steps


STEPS = directions()
DIRS = len(STEPS)
NEAR = 12


def partner(sub, step):
    summed = [BITS[sub][c] + step[c] for c in range(3)]
    return BITS.index(tuple(v % 2 for v in summed)), tuple(v // 2 for v in summed)


def site_table():
    plain, shifted, table = [], [], {}
    for sub in range(4):
        for y in range(2):
            plain.append((0, 0, y, sub))
    for sub in range(4):
        for y in range(2):
            for d, step in enumerate(STEPS):
                other, off = partner(sub, step)
                key = (off[2], off[0], y + off[1], other)
                table[(sub, y, d)] = key
                base = (0,) + key[1:]
                if base not in plain:
                    plain.append(base)
                if key[0] != 0 and key not in shifted:
                    shifted.append(key)
    return plain, shifted, table


PLAIN, SHIFTED, TABLE = site_table()
ROWS = PLAIN + SHIFTED
INDEX = {key: i for i, key in enumerate(ROWS)}
Y_LOW, Y_HIGH = -1, 2


def bring_kernel(own_in, alive_in, after, own, alive):
    own[...] = own_in[...]
    alive[...] = alive_in[...]


def fill_table(table):
    for j in range(8):
        for d in range(DIRS):
            table[j, d] = INDEX[TABLE[(j // 2, j % 2, d)]]


def even(axis):
    return lax.rem(lax.axis_index("gb" if axis == "gy" else axis), 2) == 0


def source(key, channels, own, xa, xb, ya, yb, ca, cb):
    _, x, y, sub = key
    if x == 0 and 0 <= y < 2:
        return own[sub * 2 + y]
    if 0 <= y < 2:
        j = sub * 2 + y
        return jnp.where(even("gx") == (x > 0), xa[j], xb[j])
    if x == 0:
        first, second, place = ya, yb, sub * channels
    else:
        first, second, place = ca, cb, 0 if x < 0 else channels
    part = slice(place, place + channels)
    return jnp.where(even("gy") == (y > 0), first[part, :], second[part, :])


def column_of(key):
    sz, x, y, sub = key
    group = {(-1, 0): 1, (1, 0): 2, (0, -1): 3, (0, 1): 4, (0, 0): 0}[
        (x, 0 if 0 <= y < 2 else (-1 if y < 0 else 1))
    ]
    return group * 16 + (0 if sz == 1 else 8) + sub * 2 + y % 2


CORNER = {}
for _key in PLAIN:
    if _key[1] != 0 and not 0 <= _key[2] < 2:
        CORNER[(_key[1], _key[2])] = _key[3]


def call(kernel, outs, args, scratch=(), hbm=(), hbm_outs=(), smem_outs=(), name=None, limit=vmem_bytes):
    outs = [s + (jnp.float32,) if isinstance(s[-1], int) else s for s in outs]
    spaces = [
        pltpu.HBM if i in hbm_outs else pltpu.SMEM if i in smem_outs else pltpu.VMEM
        for i in range(len(outs))
    ]
    return pl.pallas_call(
        kernel,
        out_shape=tuple(jax.ShapeDtypeStruct(s[:-1], s[-1]) for s in outs),
        in_specs=[
            pl.BlockSpec(memory_space=pltpu.HBM if i in hbm else pltpu.VMEM)
            for i in range(len(args))
        ],
        out_specs=tuple(pl.BlockSpec(memory_space=space) for space in spaces),
        scratch_shapes=list(scratch),
        compiler_params=pltpu.CompilerParams(vmem_limit_bytes=limit),
        name=name,
    )(*args)


def own_rows_kernel(
    trial_hbm, shift_hbm, species_hbm, lists_hbm, counts_hbm,
    own, low, high, columns, alive, trial, shift, species, lists, counts, sems,
):
    copies = [
        pltpu.make_async_copy(shift_hbm, shift, sems.at[0]),
        pltpu.make_async_copy(species_hbm, species, sems.at[1]),
    ]
    for c in range(3):
        part = pl.ds(c * VEC * 8, VEC * 8)
        copies.append(pltpu.make_async_copy(trial_hbm.at[part], trial.at[part], sems.at[2 + c]))
    copies.append(pltpu.make_async_copy(lists_hbm, lists, sems.at[5]))
    copies.append(pltpu.make_async_copy(counts_hbm, counts, sems.at[6]))
    for copy in copies:
        copy.start()

    def small(j, carry):
        for c in range(3):
            own[j, CH + c : CH + c + 1, :] = shift[c, pl.ds(j, 1), :]
        own[j, CH + 3 : CH + 4, :] = species[pl.ds(j, 1), :].astype(jnp.float32)
        own[j, CH + 4 : CHG, :] = jnp.zeros((4, LANES), jnp.float32)
        return carry

    copies[0].wait()
    copies[1].wait()
    lax.fori_loop(0, 8, small, 0)
    for c in range(3):

        def large(j, carry):
            own[j, c * VEC : (c + 1) * VEC, :] = trial[pl.ds(c * VEC * 8 + j, VEC, stride=8), :]
            return carry

        copies[2 + c].wait()
        lax.fori_loop(0, 8, large, 0)
    for sub in range(4):
        part = slice(sub * CHG, (sub + 1) * CHG)
        low[part, :] = jnp.where(even("gy"), own[sub * 2], own[sub * 2 + 1])
        high[part, :] = jnp.where(even("gy"), own[sub * 2 + 1], own[sub * 2])
    columns[...] = edge_columns(CHG, own)
    copies[5].wait()
    copies[6].wait()
    row = lax.broadcasted_iota(jnp.int32, (8, LANES), 0)
    lane = lax.broadcasted_iota(jnp.int32, (8, LANES), 1)
    sub, y = row // 2, row % 2
    live = counts[...]
    listed = [jnp.where(m < live, lists[m], -1) for m in range(lists.shape[0])]
    for i, step in enumerate(STEPS[NEAR:]):
        off = [v // 2 for v in step]
        expected = ((sub * 3 + 1 + off[0]) * 4 + y + 1 + off[1]) * 130 + lane + 1 + off[2]
        found = listed[0] == expected
        for m in range(1, len(listed)):
            found = found | (listed[m] == expected)
        alive[i] = found.astype(jnp.float32)


def edge_columns(channels, own):
    lane = lax.broadcasted_iota(jnp.int32, (channels, LANES), 1)
    total = jnp.zeros((channels, LANES), jnp.float32)
    for j in range(8):
        row = own[j]
        total = jnp.where(lane == j, pltpu.roll(row, j, axis=1) if j else row, total)
        total = jnp.where(lane == 8 + j, pltpu.roll(row, 9 + j, axis=1), total)
    full = jnp.concatenate([total, jnp.zeros((LANES - channels, LANES), jnp.float32)], 0)
    return full.T[:16]


def gather_rows(sites, channels, own, xa, xb, ya, yb, ca, cb, xca, xcb, zc):
    lane = lax.broadcasted_iota(jnp.int32, (channels, LANES), 1)
    for i, key in enumerate(PLAIN):
        sites[i] = source(key, channels, own, xa, xb, ya, yb, ca, cb)
    groups = [zc[...]]
    for up in (False, True):
        groups.append(jnp.where(even("gx") == up, xca[...], xcb[...]))
    for up in (False, True):
        side = slice(2 * channels, 2 * channels + 16)
        groups.append(jnp.where(even("gy") == up, ca[side, :], cb[side, :]))
    groups.append(jnp.zeros((LANES - 80, LANES), jnp.float32))
    columns = jnp.concatenate(groups, 0).T[:channels]
    for key in SHIFTED:
        turn, edge = (LANES - 1, LANES - 1) if key[0] == 1 else (1, 0)
        moved = pltpu.roll(sites[INDEX[(0,) + key[1:]]], turn, axis=1)
        by = (edge - column_of(key)) % LANES
        column = pltpu.roll(columns, by, axis=1) if by else columns
        sites[INDEX[key]] = jnp.where(lane == edge, column, moved)


def site_params(species):
    alloy = (species == 1.0).astype(jnp.float32)
    return 0.1 - 0.03 * alloy, 3.0 - 0.8 * alloy, 0.35 - 0.05 * alloy


NCOEF = 13


def tangent_kernel(
    own, xa, xb, ya, yb, ca, cb, xca, xcb, zc, alive,
    carried, low, high, columns, coef, sites, table, geo, slope,
):
    fill_table(table)
    gather_rows(sites, CHG, own, xa, xb, ya, yb, ca, cb, xca, xcb, zc)

    def place(j, carry):
        for d in range(DIRS):
            geo[pl.ds(d * 64 + j, 8, stride=8), :] = sites[table[j, d], CH:CHG, :]
        geo[pl.ds(DIRS * 64 + j, 8, stride=8), :] = own[j, CH:CHG, :]
        return carry

    lax.fori_loop(0, 8, place, 0)

    def quantity(d, n):
        return geo[d * 64 + n * 8 : d * 64 + n * 8 + 8, :]

    here = [quantity(DIRS, c) for c in range(3)]
    amp_here, embedding, pair_here = site_params(quantity(DIRS, 3))
    rho = jnp.zeros((8, LANES), jnp.float32)
    for d, step in enumerate(STEPS):
        amp, _, pair = site_params(quantity(d, 3))
        apart = [0.5 * lattice * step[c] + quantity(d, c) - here[c] for c in range(3)]
        distance = jnp.sqrt(apart[0] * apart[0] + apart[1] * apart[1] + apart[2] * apart[2])
        living = alive[d - NEAR] if d >= NEAR else 1.0
        inverse = 1.0 / distance
        unit = [v * inverse for v in apart]
        scaled = distance / nearest - 1.0
        density = living * jnp.exp(-density_rate * scaled)
        dens1 = -(density_rate / nearest) * density
        dens2 = (density_rate / nearest) ** 2 * density
        potential = living * pair_here * pair * jnp.exp(-repulse_rate * scaled)
        pot1 = -(repulse_rate / nearest) * potential
        pot2 = (repulse_rate / nearest) ** 2 * potential
        rho = rho + amp * density
        both = amp * dens1
        values = unit + [both * v for v in unit]
        values += [
            pot2 - pot1 * inverse, dens2 - dens1 * inverse, pot1 * inverse, dens1 * inverse,
            both, amp_here * dens1, amp,
        ]
        for n, value in enumerate(values):
            coef[d * NCOEF + n] = value
    root = jnp.sqrt(rho)
    slope[0] = -embedding / (2.0 * root)
    slope[1] = embedding / (4.0 * rho * root)

    def tangents(j, carry):
        mine = [own[j, q * 8 : q * 8 + 8, :] for q in range(12)]
        total = [jnp.zeros((8, LANES), jnp.float32) for _ in range(4)]
        for d in range(DIRS):
            at = table[j, d]
            weight = [coef[d * NCOEF + 3 + c, pl.ds(j, 1), :] for c in range(3)]
            for k in range(4):
                for c in range(3):
                    q = c * 4 + k
                    total[k] = total[k] + weight[c] * (mine[q] - sites[at, q * 8 : q * 8 + 8, :])
        scale = slope[1, pl.ds(j, 1), :]
        for k in range(4):
            carried[j, k * 8 : k * 8 + 8, :] = total[k] * scale
        carried[j, VEC : VEC + 1, :] = slope[0, pl.ds(j, 1), :]
        carried[j, VEC + 1 : WCH, :] = jnp.zeros((WCH - VEC - 1, LANES), jnp.float32)
        return carry

    lax.fori_loop(0, 8, tangents, 0)
    for s in range(4):
        part = slice(s * WCH, (s + 1) * WCH)
        low[part, :] = jnp.where(even("gy"), carried[s * 2], carried[s * 2 + 1])
        high[part, :] = jnp.where(even("gy"), carried[s * 2 + 1], carried[s * 2])
    columns[...] = edge_columns(WCH, carried)


def split(value):
    high = value.astype(jnp.bfloat16)
    return high, (value - high.astype(jnp.float32)).astype(jnp.bfloat16)


def mask_iota():
    row = lax.broadcasted_iota(jnp.int32, (VEC, VEC), 0)
    column = lax.broadcasted_iota(jnp.int32, (VEC, VEC), 1)
    return row, column


def packed(gram, mixed, energy):
    row, column = mask_iota()
    first = jnp.where(row <= column, gram, energy)
    even = 0.5 * (mixed + mixed.T)
    diagonal = jnp.sum(jnp.where(row == column, energy, 0.0), axis=1, keepdims=True)
    second = jnp.where(row <= column, even, jnp.where(row == column + 1, diagonal, 0.0))
    corner = jnp.broadcast_to(diagonal[0:1, :], (VEC, VEC))
    second = jnp.where((row == VEC - 1) & (column == 0), corner, second)
    half = VEC // 2
    return jnp.concatenate([first[:half], second[:half], first[half:], second[half:]], 1)


def unpacked(block):
    row, column = mask_iota()
    first = jnp.concatenate([block[:, :VEC], block[:, 2 * VEC : 3 * VEC]], 0)
    second = jnp.concatenate([block[:, VEC : 2 * VEC], block[:, 3 * VEC :]], 0)
    diagonal = jnp.sum(jnp.where(row == column + 1, second, 0.0), axis=1, keepdims=True)
    corner = jnp.broadcast_to(second[VEC - 1 :, 0:1], (VEC, 1))
    diagonal = jnp.where(row[:, 0:1] == 0, corner, diagonal)
    gram = jnp.where(row <= column, first, first.T)
    mixed = jnp.where(row <= column, second, second.T)
    energy = jnp.where(row == column, diagonal, jnp.where(row > column, first, first.T))
    return gram, mixed, energy


def image_kernel(
    own, sites, coef, w_own, w_xa, w_xb, w_ya, w_yb, w_ca, w_cb, w_xca, w_xcb, w_zc,
    local, pieces, table, even, odd, slopes, geo, mix, sums,
):
    fill_table(table)
    gather_rows(slopes, WCH, w_own, w_xa, w_xb, w_ya, w_yb, w_ca, w_cb, w_xca, w_xcb, w_zc)

    def place(j, carry):
        for d in range(DIRS):
            geo[d, pl.ds(j, 1), :] = slopes[table[j, d], VEC : VEC + 1, :]
        geo[DIRS, pl.ds(j, 1), :] = w_own[j, VEC : VEC + 1, :]
        geo[DIRS + 1, pl.ds(j, 1), :] = own[j, CH + 3 : CH + 4, :]
        return carry

    lax.fori_loop(0, 8, place, 0)
    slope_here = geo[DIRS]
    amp_here, _, _ = site_params(geo[DIRS + 1])
    lean = [jnp.zeros((8, LANES), jnp.float32) for _ in range(3)]
    for d in range(DIRS):
        mixing = slope_here * coef[d * NCOEF + 12] + geo[d] * amp_here
        mix[d * 2] = coef[d * NCOEF + 6] + mixing * coef[d * NCOEF + 7]
        mix[d * 2 + 1] = coef[d * NCOEF + 8] + mixing * coef[d * NCOEF + 9]
        lean = [lean[c] + coef[d * NCOEF + c] * coef[d * NCOEF + 10] for c in range(3)]
    for c in range(3):
        geo[c] = lean[c]

    sums[...] = jnp.zeros_like(sums)
    blocks = [(c, k) for c in range(3) for k in range(4)]

    def rows(j, wide_ref):
        mine = {b: own[j, (b[0] * 4 + b[1]) * 8 : (b[0] * 4 + b[1]) * 8 + 8, :] for b in blocks}
        total = {}
        for c in range(3):
            leaning = geo[c, pl.ds(j, 1), :]
            for k in range(4):
                total[(c, k)] = leaning * w_own[j, k * 8 : k * 8 + 8, :]
        for d in range(DIRS):
            at = table[j, d]
            unit = [coef[d * NCOEF + c, pl.ds(j, 1), :] for c in range(3)]
            radial = mix[d * 2, pl.ds(j, 1), :]
            across = mix[d * 2 + 1, pl.ds(j, 1), :]
            home = coef[d * NCOEF + 11, pl.ds(j, 1), :]
            for k in range(4):
                apart = [
                    mine[(c, k)] - sites[at, (c * 4 + k) * 8 : (c * 4 + k) * 8 + 8, :]
                    for c in range(3)
                ]
                along = unit[0] * apart[0] + unit[1] * apart[1] + unit[2] * apart[2]
                push = radial * along + home * slopes[at, k * 8 : k * 8 + 8, :]
                for c in range(3):
                    total[(c, k)] = total[(c, k)] + unit[c] * push + across * apart[c]
        wide = []
        for c in range(3):
            both = jnp.concatenate(
                [total[(c, k)] for k in range(4)] + [own[j, c * VEC : (c + 1) * VEC, :]], 0
            )
            wide.append(jnp.concatenate(split(both), 0))
        wide = jnp.concatenate(wide, 1)
        pieces[j] = wide
        wide_ref[...] = wide

    def products(wide_ref):
        wide = wide_ref[...]
        sums[...] += lax.dot_general(
            wide, wide, (((1,), (1,)), ((), ())), preferred_element_type=jnp.float32
        )

    def pair(i, carry):
        products(odd)
        rows(2 * i, even)
        products(even)
        rows(2 * i + 1, odd)
        return carry

    odd[...] = jnp.zeros_like(odd)
    lax.fori_loop(0, 4, pair, 0)
    products(odd)
    whole = sums[...]
    folded = whole[: 2 * VEC] + whole[2 * VEC :]
    folded = folded[:, : 2 * VEC] + folded[:, 2 * VEC :]
    block = packed(folded[VEC:, VEC:], folded[VEC:, :VEC], folded[:VEC, :VEC])
    for i in range(local.shape[0]):
        local[i] = block


def add_kernel(parts, out):
    total = parts[0]
    for i in range(1, parts.shape[0]):
        total = total + parts[i]
    for i in range(out.shape[0]):
        out[i] = total


def factor(gram):
    row, column = mask_iota()
    work = jnp.concatenate(
        [gram, (row == column).astype(jnp.float32), jnp.zeros((VEC, 2 * VEC), jnp.float32)], 1
    )
    below = lax.broadcasted_iota(jnp.int32, (VEC, LANES), 0)
    pivots = jnp.zeros((VEC, LANES), jnp.float32)
    for k in range(0, VEC, 4):
        sides = [jnp.broadcast_to(work[:, k + p : k + p + 1], (VEC, LANES)) for p in range(4)]
        tops = [work[k + p : k + p + 1, :] for p in range(4)]
        for p in range(4):
            at = k + p
            pivots = jnp.where(below == at, sides[p], pivots)
            ratio = jnp.where(below > at, sides[p] * (1.0 / sides[p][at : at + 1, :]), 0.0)
            for q in range(p + 1, 4):
                tops[q] = tops[q] - ratio[k + q : k + q + 1, :] * tops[p]
                sides[q] = sides[q] - ratio * sides[p][k + q : k + q + 1, :]
            work = work - ratio * tops[p]
    return (work * (1.0 / jnp.sqrt(pivots)))[:, VEC : 2 * VEC]


def exact(a, b, dims):
    return lax.dot_general(
        a, b, (dims, ((), ())), precision=lax.Precision.HIGHEST, preferred_element_type=jnp.float32
    )


def three_products(a, b, dims):
    high_a, low_a = split(a)
    high_b, low_b = split(b)
    left = jnp.concatenate([high_a, high_a, low_a], dims[0][0])
    right = jnp.concatenate([high_b, low_b, high_b], dims[1][0])
    return lax.dot_general(left, right, (dims, ((), ())), preferred_element_type=jnp.float32)


def residual_kernel(
    count_all, parts, pieces, residual_hbm, projected, rms, lost, here, residual, sems
):
    total = parts[0]
    for i in range(1, parts.shape[0]):
        total = total + parts[i]
    gram, mixed, energy = unpacked(total / count_all)
    inverse = factor(gram)
    turned = exact(inverse, jnp.concatenate([mixed, energy], 1), ((1,), (0,)))
    raw = three_products(turned[:, :VEC], inverse, ((1,), (1,)))
    sym = 0.5 * (raw + raw.T)
    projected[...] = sym
    right = three_products(sym, inverse, ((1,), (0,)))
    high, low = split(jnp.concatenate([inverse, -right], 1))
    left = jnp.concatenate([high, high, low], 1)
    total = jnp.zeros((VEC, LANES), jnp.float32)
    copies = []
    for c in range(3):
        for j in range(8):
            block = pieces[j, :, c * LANES : (c + 1) * LANES]
            value = jnp.dot(
                left,
                jnp.concatenate([block, block[: 2 * VEC]], 0),
                preferred_element_type=jnp.float32,
            )
            residual[pl.ds(c * VEC * 8 + j, VEC, stride=8), :] = value
            total = total + value * value
        part = pl.ds(c * VEC * 8, VEC * 8)
        copies.append(pltpu.make_async_copy(residual.at[part], residual_hbm.at[part], sems.at[c]))
        copies[-1].start()
    norms = jnp.sum(turned[:, VEC:] * inverse, axis=1, keepdims=True)
    left_over = norms - jnp.sum(sym * sym, axis=1, keepdims=True)
    wide = jnp.concatenate(
        [
            jnp.broadcast_to(jnp.sqrt(left_over + epsilon), (VEC, LANES)),
            jnp.broadcast_to(jnp.sum(total, axis=1, keepdims=True), (VEC, LANES)),
            jnp.zeros((LANES - 2 * VEC, LANES), jnp.float32),
        ],
        0,
    ).T
    rms[...] = wide[0:1, :VEC]
    here[...] = wide[0:1, VEC : 2 * VEC]
    kept = jnp.where(left_over > 0.05 * norms, 0, 1)
    lost[0, 0] = jnp.max(kept)
    for copy in copies:
        copy.wait()


def met(first, second, axis):
    axes = ("ga", "gb") if axis == "gy" else (axis,)
    peers = peers_of(axes)
    pairs = [(i, i ^ 1) for i in range(peers)]
    others = [(i, (i + 1) % peers if i % 2 else (i - 1) % peers) for i in range(peers)]
    return lax.ppermute(first, axes, pairs), lax.ppermute(second, axes, others)


def exchanged(parts, axes):
    return lax.all_to_all(parts, axes, 0, 0, tiled=False)


def halo(channels, own, low, high, columns):
    ya, yb = met(high, low, "gy")
    za, zb = met(columns, columns, "gz")
    xa, xb = met(own, own, "gx")
    row = lax.broadcasted_iota(jnp.int32, columns.shape, 0)
    zc = jnp.where((row < 8) == even("gz"), za, zb)

    def corners(side, y):
        below, above = CORNER[(-1, side)] * 2 + y, CORNER[(1, side)] * 2 + y
        return [
            jnp.where(even("gx"), xb[below], xa[below]),
            jnp.where(even("gx"), xa[above], xb[above]),
        ]

    up, down = corners(Y_LOW, 1), corners(Y_HIGH, 0)
    first = [jnp.where(even("gy"), u, d) for u, d in zip(up, down)]
    second = [jnp.where(even("gy"), d, u) for u, d in zip(up, down)]
    ca, cb = met(jnp.concatenate(first + [zc], 0), jnp.concatenate(second + [zc], 0), "gy")
    xca, xcb = met(zc, zc, "gx")
    return xa, xb, ya, yb, ca, cb, xca, xcb, zc


FIRST, SECOND = ("gx",), ("ga", "gb", "gz")


def peers_of(axes):
    return math.prod(lax.axis_size(axis) for axis in axes)


def body(trial_block, site_shift, species, neighbours, counts):
    first, second = peers_of(FIRST), peers_of(SECOND)
    count_all = 3.0 * 1024 * first * second
    vmem = lambda shape, dtype=jnp.float32: pltpu.VMEM(shape, dtype)
    lists = neighbours.reshape(-1, 8, LANES)
    edge = (16, LANES)
    table = pltpu.SMEM((8, DIRS), jnp.int32)
    own, low, high, columns, alive = call(
        own_rows_kernel,
        ((8, CHG, LANES), (4 * CHG, LANES), (4 * CHG, LANES), edge, (DIRS - NEAR, 8, LANES)),
        (
            trial_block.reshape(CH * 8, LANES),
            site_shift.reshape(3, 8, LANES),
            species.reshape(8, LANES),
            lists,
            counts.reshape(8, LANES),
        ),
        scratch=[
            vmem((CH * 8, LANES)), vmem((3, 8, LANES)), vmem((8, LANES), jnp.int32),
            vmem(lists.shape, jnp.int32), vmem((8, LANES), jnp.int32),
            pltpu.SemaphoreType.DMA((7,)),
        ],
        hbm=(0, 1, 2, 3, 4),
        name="own_rows",
        limit=60 * 1024 * 1024,
    )
    around = halo(CHG, own, low, high, columns)
    own, alive = call(
        bring_kernel, (own.shape, alive.shape), (own, alive, around[-1]), name="bring"
    )
    carried, low_w, high_w, columns_w, coef, sites = call(
        tangent_kernel,
        (
            (8, WCH, LANES), (4 * WCH, LANES), (4 * WCH, LANES), edge, (DIRS * NCOEF, 8, LANES),
            (len(ROWS), CHG, LANES),
        ),
        (own,) + around + (alive,),
        scratch=[table, vmem(((DIRS + 1) * 64, LANES)), vmem((2, 8, LANES))],
        name="tangents",
    )
    around_w = halo(WCH, carried, low_w, high_w, columns_w)
    local, pieces = call(
        image_kernel,
        ((first, VEC // 2, LANES), (8, 4 * VEC, 3 * LANES, jnp.bfloat16)),
        (own, sites, coef, carried) + around_w,
        scratch=[
            table, vmem((4 * VEC, 3 * LANES), jnp.bfloat16),
            vmem((4 * VEC, 3 * LANES), jnp.bfloat16), vmem((len(ROWS), WCH, LANES)),
            vmem((DIRS + 2, 8, LANES)), vmem((DIRS * 2, 8, LANES)), vmem((4 * VEC, 4 * VEC)),
        ],
        name="images",
    )
    (group,) = call(
        add_kernel, ((second, VEC // 2, LANES),), (exchanged(local, FIRST),), name="group_sum"
    )

    def kernel(*refs):
        residual_kernel(count_all, *refs)

    residual, projected, rms, lost, here = call(
        kernel,
        ((CH * 8, LANES), (VEC, VEC), (1, VEC), (1, 1, jnp.int32), (1, VEC)),
        (exchanged(group, SECOND), pieces),
        scratch=[vmem((CH * 8, LANES)), pltpu.SemaphoreType.DMA((3,))],
        hbm_outs=(0,),
        smem_outs=(3,),
        name="residuals",
    )
    rms = lax.cond(
        lost[0, 0] != 0,
        lambda: jnp.sqrt(lax.psum(here, FIRST + SECOND) / count_all + epsilon),
        lambda: rms,
    )
    return residual.reshape(trial_block.shape), projected, rms.reshape(VEC)


def solution(mesh):
    grid = mesh.devices
    halves = jax.sharding.Mesh(
        grid.reshape(grid.shape[0], 2, grid.shape[1] // 2, grid.shape[2]), ("gx", "ga", "gb", "gz")
    )
    cells = ("gx", ("ga", "gb"), "gz")
    placed = (
        P(None, None, *cells),
        P(None, None, *cells),
        P(None, *cells),
        P(None, None, *cells),
        P(None, *cells),
    )
    return jax.shard_map(
        body,
        mesh=halves,
        in_specs=placed,
        out_specs=(P(None, None, *cells), P(), P()),
        check_vma=False,
    )
```
